256 devices in a mesh: band: 64 (over z, x_lo, y), pc: 4 (over x_hi, core).
Axes of the slice: x: 4 (x_hi: 2, x_lo: 2; x = x_hi * 2 + x_lo), y: 4, z: 8, core: 2. Of those that a mesh axis runs over, the one named last changes fastest.
Arguments:
- planes: bfloat16 [3, 256, 256, 256], P(None, 'band', 'pc'), may hold values from -15 to 15
- cotangent: bfloat16 [3, 256, 256, 256], P(None, 'band', 'pc'), may hold values from -6 to 6
- conv_weight: bfloat16 [9, 256, 256], P(None, 'pc'), may hold values from -0.125 to 0.125
- context_gain: bfloat16 [256], P('pc'), may hold values from 0.5 to 1.5
- step_index: int32 [1], replicated, may hold values from 0 to 999
Outputs:
- block_out: bfloat16 [3, 256, 256, 256], P(None, 'band', 'pc')
- input_grad: bfloat16 [3, 256, 256, 256], P(None, 'band', 'pc')
- weight_grad: float32 [9, 256, 256], P(None, 'pc', 'band')
The draws below stay inside these ranges and needn't reach their ends.
All inputs are finite; a program needn't handle non-finite values.
Results may differ from the reference program's by a relative error of at most 0.0027.
The reference program's roundings to bfloat16 on the way (of `grad_z`) count: a program that leaves them out, or rounds other values in their place, can miss the bound.
Values may be sent and summed in bfloat16 or wider, within the bound.
A program may use at most 64 MiB of HBM per device.

```python
import math
import jax
import jax.numpy as jnp
from jax import lax

C = 256
KS = 9
R = 256


def draw_planes(key, part):
    key = jax.random.fold_in(key, 11)
    base_key, offset_key, row_key, col_key = jax.random.split(key, 4)
    ramp = 1.0 + 2.0 * jnp.arange(R, dtype=jnp.float32) / (R - 1)
    offsets = 0.4 * jax.random.uniform(offset_key, (3, 1, C, 1), jnp.float32, -1.0, 1.0)
    base = jnp.clip(jax.random.normal(base_key, (3, R, C, R), jnp.float32), -6.0, 6.0)
    row_scale = jax.random.uniform(row_key, (3, R, 1, 1), jnp.float32, 0.5, 1.5)
    col_scale = jax.random.uniform(col_key, (3, 1, 1, R), jnp.float32, 0.5, 1.5)
    row_factor = row_scale * ramp[None, :, None, None]
    col_factor = col_scale * ramp[None, None, None, :]
    return (base + offsets * row_factor * col_factor).astype(jnp.bfloat16)


def block_levels(own_key, dims, cuts, smallest, high):
    loudness = 1.0
    for dim, shards_of in cuts:
        steps = jax.random.uniform(jax.random.fold_in(jax.random.fold_in(own_key, 6), dim), (shards_of,), jnp.float32, smallest / len(cuts), high / len(cuts))
        loudness = loudness * jnp.repeat(jnp.exp(steps), dims[dim] // shards_of).reshape((-1,) + (1,) * (len(dims) - 1 - dim))
    return loudness


def centred(own_key, shape, scale, reach, pieces=(), kind=jnp.bfloat16):
    array = scale * jax.random.normal(own_key, shape, jnp.float32)
    if pieces:
        array = array * block_levels(own_key, shape, pieces, -0.22, 0.18)
    return jnp.clip(array, -reach, reach).astype(kind)


def setup_inputs(seed: int = 0) -> dict:
    keys = jax.random.split(jax.random.key(seed), 6)
    return {
        "planes": draw_planes(jax.random.fold_in(keys[5], 71), 0),
        "cotangent": centred(keys[1], (3, R, C, R), 1.0, 6.0, ((1, 64), (2, 4))),
        "conv_weight": centred(keys[2], (KS, C, C), (9 * C) ** -0.5, 0.125, ((1, 4),)),
        "context_gain": jnp.clip(0.5 + 1.0 * jax.random.uniform(keys[3], (C,), jnp.float32) ** block_levels(keys[3], (C,), ((0, 4),), -0.2, 0.2), 0.5, 1.5).astype(jnp.bfloat16),
        "step_index": jax.random.randint(keys[4], (1,), 0, 1000).astype(jnp.int32),
    }


def time_embed(step_index, channel_ids, channels):
    moment = step_index[0].astype(jnp.float32)
    frequency = jnp.exp(-math.log(10000.0) * (2 * (channel_ids // 2)).astype(jnp.float32) / channels)
    phase = moment * frequency
    return jnp.where(channel_ids % 2 == 0, jnp.sin(phase), jnp.cos(phase))


def context_full(values):
    row_means = jnp.mean(values, axis=3)
    col_means = jnp.mean(values, axis=1)
    plane_one = row_means[1][:, :, None] + jnp.transpose(row_means[2])[None]
    plane_two = row_means[0][:, :, None] + col_means[2][None]
    plane_three = jnp.transpose(col_means[0])[:, :, None] + col_means[1][None]
    return jnp.stack([plane_one, plane_two, plane_three])


def reference(planes, cotangent, conv_weight, context_gain, step_index):
    inputs = planes.astype(jnp.float32)
    weights = conv_weight.astype(jnp.float32)
    gain_vec = context_gain.astype(jnp.float32)[None, None, :, None]
    time_vec = time_embed(step_index, jnp.arange(C, dtype=jnp.int32), C)[None, None, :, None]
    padded = jnp.pad(inputs, ((0, 0), (1, 1), (0, 0), (1, 1)))

    def conv_plane(plane):
        total = jnp.zeros((R, C, R), jnp.float32)
        for row_tap in range(3):
            for col_tap in range(3):
                window = plane[row_tap:row_tap + R, :, col_tap:col_tap + R]
                total = total + jnp.einsum("oc,icj->ioj", weights[3 * row_tap + col_tap], window)
        return total

    pre_act = lax.map(conv_plane, padded) + gain_vec * context_full(inputs) + time_vec
    block_out = (inputs + jax.nn.silu(pre_act)).astype(jnp.bfloat16)
    sigma_z = jax.nn.sigmoid(pre_act)
    grad_z = (cotangent.astype(jnp.float32) * sigma_z * (1.0 + pre_act * (1.0 - sigma_z))).astype(jnp.bfloat16)
    grad_values = grad_z.astype(jnp.float32)
    grad_padded = jnp.pad(grad_values, ((0, 0), (1, 1), (0, 0), (1, 1)))

    def back_plane(plane):
        total = jnp.zeros((R, C, R), jnp.float32)
        for row_tap in range(3):
            for col_tap in range(3):
                window = plane[2 - row_tap:2 - row_tap + R, :, 2 - col_tap:2 - col_tap + R]
                total = total + jnp.einsum("oc,ioj->icj", weights[3 * row_tap + col_tap], window)
        return total

    conv_back = lax.map(back_plane, grad_padded)
    input_grad = (cotangent.astype(jnp.float32) + conv_back + context_full(gain_vec * grad_values)).astype(jnp.bfloat16)

    def weight_plane(pair):
        grad_plane, plane = pair
        terms = []
        for row_tap in range(3):
            for col_tap in range(3):
                window = plane[row_tap:row_tap + R, :, col_tap:col_tap + R]
                terms.append(jnp.einsum("ioj,icj->oc", grad_plane, window))
        return jnp.stack(terms)

    weight_grad = jnp.sum(lax.map(weight_plane, (grad_values, padded)), axis=0)
    return block_out, input_grad, weight_grad
```

```python
import math

import jax
import jax.numpy as jnp
from jax import lax
from jax.experimental import pallas as pl
from jax.experimental.pallas import tpu as pltpu
from jax.sharding import PartitionSpec as P

C = 256
MESH = pl.DeviceIdType.MESH
BANDS = 64
F32 = jnp.float32
BF16 = jnp.bfloat16


def time_embed(step_index, channel_ids, channels):
    moment = step_index[0].astype(jnp.float32)
    frequency = jnp.exp(
        -math.log(10000.0) * (2 * (channel_ids // 2)).astype(jnp.float32) / channels
    )
    phase = moment * frequency
    return jnp.where(channel_ids % 2 == 0, jnp.sin(phase), jnp.cos(phase))


def shifted(values, step):
    if step == 0:
        return values
    columns = lax.broadcasted_iota(jnp.int32, values.shape, 1)
    width = values.shape[1]
    rolled = pltpu.roll(values, step % width, 1)
    edge = 0 if step == 1 else width - 1
    return jnp.where(columns == edge, 0.0, rolled)


def kernel(
    planes, cotangent, weights, gain, time_vec,
    block_out, input_grad, weight_grad,
    rows, cot, wf, wa, wb, pre, stacks, out_a, out_b,
    sums, row_sums, ra, av, rb, gb, gc,
    wacc, wsend, rz, rv, rm,
    load_sem, send_sem, recv_sem, ar_send, ar_recv, w_send, w_recv, wg_send, wg_recv, store_sem,
):
    b = lax.axis_index("band")
    p = lax.axis_index("pc")
    z, m = b // 8, b % 8
    h, k = p // 2, p % 2
    across = (b, (1 - h) * 2 + k)
    beside = (b, h * 2 + (1 - k))
    above, below = (b - 1, p), (b + 1, p)
    has_above, has_below = b > 0, b < BANDS - 1

    def m_peer(step):
        return (z * 8 + (m + step) % 8, p)

    def z_peer(step):
        return (((z + step) % 8) * 8 + m, p)

    def load(number, src, dst):
        return pltpu.make_async_copy(src, dst, load_sem.at[number])

    loads = [load(i, planes.at[i], rows.at[0, i, pl.ds(1, 4), h, k]) for i in range(3)]
    loads.append(load(3, cotangent, cot))
    for tap_row in range(3):
        for tap_col in range(3):
            loads.append(
                load(
                    4 + 3 * tap_row + tap_col,
                    weights.at[3 * tap_row + tap_col],
                    wf.at[pl.ds(tap_col * 64, 64), pl.ds(tap_row * 256, 256)],
                )
            )
    half = pl.multiple_of(h * 128, 128)
    other_half = pl.multiple_of((1 - h) * 128, 128)
    loads.append(load(13, weights.at[:, :, pl.ds(half, 128)], wa.at[:, h, k]))
    for copy in loads:
        copy.start()

    barrier = pltpu.get_barrier_semaphore()
    for step in range(1, 8):
        pl.semaphore_signal(barrier, inc=1, device_id=m_peer(step), device_id_type=MESH)
        pl.semaphore_signal(barrier, inc=1, device_id=z_peer(step), device_id_type=MESH)
    pl.semaphore_signal(barrier, inc=1, device_id=across, device_id_type=MESH)
    pl.semaphore_signal(barrier, inc=1, device_id=beside, device_id_type=MESH)
    far_above = jnp.logical_and(m == 0, has_above)
    far_below = jnp.logical_and(m == 7, has_below)

    @pl.when(far_above)
    def _():
        pl.semaphore_signal(barrier, inc=1, device_id=above, device_id_type=MESH)

    @pl.when(far_below)
    def _():
        pl.semaphore_signal(barrier, inc=1, device_id=below, device_id_type=MESH)

    pl.semaphore_wait(
        barrier, 16 + far_above.astype(jnp.int32) + far_below.astype(jnp.int32)
    )

    def piece(which, plane, kind, dst, src, target):
        return pltpu.make_async_remote_copy(
            src_ref=src,
            dst_ref=dst,
            send_sem=send_sem.at[which, plane, kind],
            recv_sem=recv_sem.at[which, plane, kind],
            device_id=target,
            device_id_type=MESH,
        )

    def incoming(which, plane, kind, dst, target=None):
        return piece(which, plane, kind, dst, dst, across if target is None else target)

    def send_own(which, plane, own=None):
        buf = rows.at[which, plane]
        body = buf.at[pl.ds(1, 4), h, k]
        src = body if own is None else own
        first = buf.at[1, h, k] if own is None else own.at[0]
        last = buf.at[4, h, k] if own is None else own.at[3]
        piece(which, plane, 0, body, src, across).start()

        @pl.when(has_above)
        def _():
            piece(which, plane, 2, buf.at[5, h, k], first, above).start()

        @pl.when(has_below)
        def _():
            piece(which, plane, 3, buf.at[0, h, k], last, below).start()

        piece(which, plane, 1, body, src, beside).start()

    def pass_on(which, plane):
        buf = rows.at[which, plane]
        body = buf.at[pl.ds(1, 4), 1 - h, k]
        incoming(which, plane, 0, body).wait_recv()

        @pl.when(has_above)
        def _():
            piece(which, plane, 5, buf.at[5, 1 - h, k], buf.at[1, 1 - h, k], above).start()

        @pl.when(has_below)
        def _():
            piece(which, plane, 6, buf.at[0, 1 - h, k], buf.at[4, 1 - h, k], below).start()

        piece(which, plane, 4, body, body, beside).start()

    def pass_rim(which, plane):
        buf = rows.at[which, plane]

        @pl.when(has_below)
        def _():
            incoming(which, plane, 2, buf.at[5, h, k]).wait_recv()
            incoming(which, plane, 5, buf.at[5, 1 - h, k]).wait_recv()
            piece(which, plane, 7, buf.at[5, :, k], buf.at[5, :, k], beside).start()

        @pl.when(has_above)
        def _():
            incoming(which, plane, 3, buf.at[0, h, k]).wait_recv()
            incoming(which, plane, 6, buf.at[0, 1 - h, k]).wait_recv()
            piece(which, plane, 8, buf.at[0, :, k], buf.at[0, :, k], beside).start()

    def arrive(which, plane):
        buf = rows.at[which, plane]
        incoming(which, plane, 1, buf.at[pl.ds(1, 4), h, 1 - k]).wait_recv()
        incoming(which, plane, 4, buf.at[pl.ds(1, 4), 1 - h, 1 - k]).wait_recv()

        @pl.when(has_below)
        def _():
            incoming(which, plane, 7, buf.at[5, :, 1 - k]).wait_recv()

        @pl.when(has_above)
        def _():
            incoming(which, plane, 8, buf.at[0, :, 1 - k]).wait_recv()

    def settle(which, plane):
        buf = rows.at[which, plane]
        body = buf.at[pl.ds(1, 4), h, k]
        for kind in (0, 1, 4):
            piece(which, plane, kind, body, body, across).wait_send()

        @pl.when(has_above)
        def _():
            for kind in (2, 5):
                piece(which, plane, kind, buf.at[5, h, k], buf.at[5, h, k], above).wait_send()
            piece(which, plane, 8, buf.at[0, :, k], buf.at[0, :, k], beside).wait_send()

        @pl.when(has_below)
        def _():
            for kind in (3, 6):
                piece(which, plane, kind, buf.at[0, h, k], buf.at[0, h, k], below).wait_send()
            piece(which, plane, 7, buf.at[5, :, k], buf.at[5, :, k], beside).wait_send()

    def ar_copy(which, stage, step, src, dst, target):
        return pltpu.make_async_remote_copy(
            src_ref=src,
            dst_ref=dst,
            send_sem=ar_send.at[which, stage, step - 1],
            recv_sem=ar_recv.at[which, stage, step - 1],
            device_id=target,
            device_id_type=MESH,
        )

    def ar_start(which):
        for step in range(1, 8):
            to = (m + step) % 8
            ar_copy(
                which, 0, step, sums.at[which, to], ra.at[which, m], m_peer(step)
            ).start()
        ra[which, m] = sums[which, m]

    def ar_second(which):
        for step in range(1, 8):
            ar_copy(which, 0, step, sums.at[which, 0], ra.at[which, (m + 8 - step) % 8], m_peer(step)).wait_recv()
        total = ra[which, 0]
        for i in range(1, 8):
            total = total + ra[which, i]
        av[which] = total
        for step in range(1, 8):
            to = (z + step) % 8
            ar_copy(which, 1, step, av.at[which, to], rb.at[which, z], z_peer(step)).start()
        rb[which, z] = av[which, z]

    def ar_third(which):
        for step in range(1, 8):
            ar_copy(which, 1, step, av.at[which, 0], rb.at[which, (z + 8 - step) % 8], z_peer(step)).wait_recv()
        total = rb[which, 0]
        for i in range(1, 8):
            total = total + rb[which, i]
        gb[which, z] = total
        for step in range(1, 8):
            ar_copy(which, 2, step, gb.at[which, z], gb.at[which, z], z_peer(step)).start()

    def ar_fourth(which):
        for step in range(1, 8):
            slot = gb.at[which, (z + 8 - step) % 8]
            ar_copy(which, 2, step, slot, slot, z_peer(step)).wait_recv()
        for step in range(1, 8):
            ar_copy(which, 3, step, gb.at[which], gc.at[which, m], m_peer(step)).start()
        gc[which, m] = gb[which]

    def ar_finish(which):
        for step in range(1, 8):
            slot = gc.at[which, (m + 8 - step) % 8]
            ar_copy(which, 3, step, slot, slot, m_peer(step)).wait_recv()

    def ar_settle(which):
        for step in range(1, 8):
            ar_copy(which, 0, step, sums.at[which, 0], ra.at[which, 0], m_peer(step)).wait_send()
            ar_copy(which, 1, step, av.at[which, 0], rb.at[which, 0], z_peer(step)).wait_send()
            ar_copy(which, 2, step, gb.at[which, 0], gb.at[which, 0], z_peer(step)).wait_send()
            ar_copy(which, 3, step, gb.at[which], gc.at[which, 0], m_peer(step)).wait_send()

    columns = lax.broadcasted_iota(jnp.int32, (64, 256), 1)

    def make_sums(which):
        for plane in range(3):
            total = None
            spread = jnp.zeros((64, 256), F32)
            for i in range(4):
                values = rows[which, plane, 1 + i, h, k].astype(F32)
                total = values if total is None else total + values
                row = jnp.sum(values, axis=1, keepdims=True)
                if plane < 2:
                    row_sums[which, plane, i] = row
                else:
                    spread = jnp.where(columns == b * 4 + i, row, spread)
            for side in range(2):
                lanes = slice(side * 128, side * 128 + 128)
                sums[which, :, plane * 2 + side] = total[:, lanes].reshape(8, 8, 128)
                if plane == 2:
                    sums[which, :, 6 + side] = spread[:, lanes].reshape(8, 8, 128)

    def totals(which, number):
        return jnp.concatenate(
            [gc[which, :, number * 2 + side].reshape(64, 128) for side in range(2)], axis=1
        )

    def context_row(which, plane, i, whole):
        if plane == 0:
            return row_sums[which, 1, i] + whole
        if plane == 1:
            return row_sums[which, 0, i] + whole
        own = jnp.sum(
            jnp.where(columns == b * 4 + i, totals(which, 0), 0.0), axis=1, keepdims=True
        )
        return own + whole

    whole_of = (3, 2, 1)

    for i in range(3):
        send_own(0, i, planes.at[i])
    for i in range(3):
        loads[i].wait()
    make_sums(0)
    ar_start(0)

    def w_copy(kind, src, dst, target):
        return pltpu.make_async_remote_copy(
            src_ref=src, dst_ref=dst, send_sem=w_send.at[kind], recv_sem=w_recv.at[kind],
            device_id=target, device_id_type=MESH,
        )

    w_copy(0, weights.at[:, :, pl.ds(other_half, 128)], wa.at[:, h, k], across).start()
    w_copy(1, weights.at[:, :, pl.ds(half, 128)], wa.at[:, h, k], beside).start()

    zero_row = jnp.zeros((2, 2, 64, 256), BF16)

    @pl.when(jnp.logical_not(has_above))
    def _():
        for which in range(2):
            for plane in range(3):
                rows[which, plane, 0] = zero_row

    @pl.when(jnp.logical_not(has_below))
    def _():
        for which in range(2):
            for plane in range(3):
                rows[which, plane, 5] = zero_row

    for copy in loads[3:]:
        copy.wait()
    for plane in range(3):
        pass_on(0, plane)
    ar_second(0)
    for plane in range(3):
        pass_rim(0, plane)
    ar_third(0)

    def convolve(which, plane, matrix, back):
        def one(i, carry):
            slab = rows[which, plane, pl.ds(i, 3)].reshape(768, 256)
            parts = jnp.dot(matrix[...], slab, preferred_element_type=F32)
            signs = (-1, 0, 1) if back else (1, 0, -1)
            total = parts[64:128]
            for tap in (0, 2):
                total = total + shifted(parts[tap * 64 : tap * 64 + 64], signs[tap])
            pre[plane, i] = total
            return carry

        lax.fori_loop(0, 4, one, 0)

    arrive(0, 0)
    convolve(0, 0, wf, False)
    ar_fourth(0)
    arrive(0, 1)
    convolve(0, 1, wf, False)
    arrive(0, 2)
    convolve(0, 2, wf, False)

    arrived = wa.at[:, 1 - h, k]
    w_copy(0, arrived, arrived, across).wait_recv()
    w_copy(2, arrived, arrived, beside).start()

    ar_finish(0)
    gain_vec = gain[...]
    time_col = time_vec[...]
    for plane in range(3):
        whole = totals(0, whole_of[plane])

        def finish(i, carry):
            context = context_row(0, plane, i, whole) * (1.0 / 256.0)
            act = pre[plane, i] + gain_vec * context + time_col
            gate = jax.nn.sigmoid(act)
            values = rows[0, plane, 1 + i, h, k].astype(F32)
            out_a[plane, i] = (values + act * gate).astype(BF16)
            grad = cot[plane, i].astype(F32) * gate * (1.0 + act * (1.0 - gate))
            rows[1, plane, 1 + i, h, k] = grad.astype(BF16)
            return carry

        lax.fori_loop(0, 4, finish, 0)
        send_own(1, plane)
        pltpu.make_async_copy(out_a.at[plane], block_out.at[plane], store_sem.at[0, plane]).start()

    make_sums(1)
    ar_start(1)

    for plane in range(3):

        def stack(i, carry):
            grad = rows[1, plane, 1 + i, h, k].astype(F32)
            for tap in range(3):
                stacks[plane, i, pl.ds(tap * 64, 64)] = shifted(grad, tap - 1).astype(BF16)
            return carry

        lax.fori_loop(0, 4, stack, 0)

    for kind, dst in ((1, wa.at[:, h, 1 - k]), (2, wa.at[:, 1 - h, 1 - k])):
        w_copy(kind, dst, dst, beside).wait_recv()
    for tap_row in range(3):
        for tap_col in range(3):
            block = wa[3 * tap_row + tap_col].reshape(256, 128).astype(F32)
            turned = jnp.transpose(block)
            turned = jnp.where(k == 0, turned[:64], turned[64:])
            wb[pl.ds(tap_col * 64, 64), pl.ds((2 - tap_row) * 256, 256)] = turned.astype(BF16)

    def weight_terms(plane):
        grads = jnp.concatenate([stacks[plane, i] for i in range(4)], axis=1)

        for tap_row in range(3):
            window = jnp.concatenate(
                [rows[0, plane, tap_row + i].reshape(256, 256) for i in range(4)], axis=1
            )
            term = lax.dot_general(
                window, grads, (((1,), (1,)), ((), ())), preferred_element_type=F32
            )
            if plane == 0:
                wacc[tap_row] = term
            else:
                wacc[tap_row] += term

    def wg_copy(stage, step, src, dst, target):
        return pltpu.make_async_remote_copy(
            src_ref=src, dst_ref=dst,
            send_sem=wg_send.at[stage, step - 1], recv_sem=wg_recv.at[stage, step - 1],
            device_id=target, device_id_type=MESH,
        )

    weight_terms(0)
    pass_on(1, 0)
    ar_second(1)
    weight_terms(1)
    pass_on(1, 1)
    ar_third(1)
    weight_terms(2)
    pass_on(1, 2)
    for i in range(8):
        part = [wacc[tap_row, pl.ds(i * 32, 32), :] for tap_row in range(3)]
        part.append(jnp.zeros((32, 64), F32))
        wsend[i] = jnp.concatenate(part, axis=1)
    for step in range(1, 8):
        to = (z + step) % 8
        wg_copy(0, step, wsend.at[to], rz.at[z], z_peer(step)).start()
    rz[z] = wsend[z]
    ar_fourth(1)
    for plane in range(3):
        pass_rim(1, plane)
    for plane in range(3):
        arrive(1, plane)
        convolve(1, plane, wb, True)
    ar_finish(1)
    for plane in range(3):
        whole = totals(1, whole_of[plane])

        def finish_back(i, carry):
            context = context_row(1, plane, i, whole) * (1.0 / 256.0)
            grad = cot[plane, i].astype(F32) + pre[plane, i] + gain_vec * context
            out_b[plane, i] = grad.astype(BF16)
            return carry

        lax.fori_loop(0, 4, finish_back, 0)
        pltpu.make_async_copy(out_b.at[plane], input_grad.at[plane], store_sem.at[1, plane]).start()

    for step in range(1, 8):
        slot = rz.at[(z + 8 - step) % 8]
        wg_copy(0, step, slot, slot, z_peer(step)).wait_recv()
    total = rz[0]
    for i in range(1, 8):
        total = total + rz[i]
    rv[...] = total.reshape(4, 8, 640)
    for step in range(1, 8):
        to = (m + step) % 8
        wg_copy(1, step, rv.at[to // 2], rm.at[m], m_peer(step)).start()
    rm[m] = rv[m // 2]
    for step in range(1, 8):
        slot = rm.at[(m + 8 - step) % 8]
        wg_copy(1, step, slot, slot, m_peer(step)).wait_recv()
    total = rm[0]
    for i in range(1, 8):
        total = total + rm[i]
    total = jnp.where(m % 2 == 0, total[:4], total[4:])
    for tap in range(9):
        weight_grad[tap] = total[:, tap * 64 : tap * 64 + 64]

    for which in range(2):
        for plane in range(3):
            settle(which, plane)
        ar_settle(which)
    for kind in range(3):
        w_copy(kind, arrived, arrived, across).wait_send()
    for step in range(1, 8):
        wg_copy(0, step, wsend.at[0], rz.at[0], z_peer(step)).wait_send()
        wg_copy(1, step, rv.at[0], rm.at[0], m_peer(step)).wait_send()
    for plane in range(3):
        pltpu.make_async_copy(out_a.at[plane], block_out.at[plane], store_sem.at[0, plane]).wait()
        pltpu.make_async_copy(out_b.at[plane], input_grad.at[plane], store_sem.at[1, plane]).wait()


def on_device(planes, cotangent, conv_weight, context_gain, step_index):
    channel_ids = lax.axis_index("pc") * 64 + jnp.arange(64, dtype=jnp.int32)
    time_vec = time_embed(step_index, channel_ids, C)[:, None]
    gain = context_gain.astype(F32)[:, None]
    any_spec = pl.BlockSpec(memory_space=pl.ANY)
    vmem = pl.BlockSpec(memory_space=pltpu.VMEM)
    dma = pltpu.SemaphoreType.DMA
    block_out, input_grad, weight_grad = pl.pallas_call(
        kernel,
        out_shape=(
            jax.ShapeDtypeStruct((3, 4, 64, 256), BF16),
            jax.ShapeDtypeStruct((3, 4, 64, 256), BF16),
            jax.ShapeDtypeStruct((9, 4, 64), F32),
        ),
        in_specs=[any_spec, any_spec, any_spec, vmem, vmem],
        out_specs=(any_spec, any_spec, vmem),
        scratch_shapes=[
            pltpu.VMEM((2, 3, 6, 2, 2, 64, 256), BF16),
            pltpu.VMEM((3, 4, 64, 256), BF16),
            pltpu.VMEM((192, 768), BF16),
            pltpu.VMEM((9, 2, 2, 64, 128), BF16),
            pltpu.VMEM((192, 768), BF16),
            pltpu.VMEM((3, 4, 64, 256), F32),
            pltpu.VMEM((3, 4, 192, 256), BF16),
            pltpu.VMEM((3, 4, 64, 256), BF16),
            pltpu.VMEM((3, 4, 64, 256), BF16),
            pltpu.VMEM((2, 8, 8, 8, 128), F32),
            pltpu.VMEM((2, 2, 4, 64, 1), F32),
            pltpu.VMEM((2, 8, 8, 8, 128), F32),
            pltpu.VMEM((2, 8, 8, 128), F32),
            pltpu.VMEM((2, 8, 8, 128), F32),
            pltpu.VMEM((2, 8, 8, 128), F32),
            pltpu.VMEM((2, 8, 8, 8, 128), F32),
            pltpu.VMEM((3, 256, 192), F32),
            pltpu.VMEM((8, 32, 640), F32),
            pltpu.VMEM((8, 32, 640), F32),
            pltpu.VMEM((4, 8, 640), F32),
            pltpu.VMEM((8, 8, 640), F32),
            dma((14,)),
            dma((2, 3, 9)),
            dma((2, 3, 9)),
            dma((2, 4, 7)),
            dma((2, 4, 7)),
            dma((3,)),
            dma((3,)),
            dma((2, 7)),
            dma((2, 7)),
            dma((2, 3)),
        ],
        compiler_params=pltpu.CompilerParams(
            collective_id=0, has_side_effects=True, vmem_limit_bytes=48 * 1024 * 1024
        ),
        name="triplane",
    )(planes, cotangent, conv_weight, gain, time_vec)
    return block_out, input_grad, jnp.transpose(weight_grad, (0, 2, 1))


def solution(mesh):
    in_specs = (
        P(None, "band", "pc", None),
        P(None, "band", "pc", None),
        P(None, "pc", None),
        P("pc"),
        P(),
    )
    out_specs = (P(None, "band", "pc", None), P(None, "band", "pc", None), P(None, "pc", "band"))
    return jax.shard_map(
        on_device, mesh=mesh, in_specs=in_specs, out_specs=out_specs, check_vma=False
    )
```

```python
import math

import jax
import jax.numpy as jnp
from jax import lax
from jax.experimental import pallas as pl
from jax.experimental.pallas import tpu as pltpu
from jax.sharding import PartitionSpec as P

C = 256
MESH = pl.DeviceIdType.MESH
BANDS = 64
VMEM_LIMIT = 60 * 1024 * 1024
WIRE = jnp.float32
F32 = jnp.float32
BF16 = jnp.bfloat16


def time_embed(step, channel_ids):
    frequency = jnp.exp(-math.log(10000.0) * (2 * (channel_ids // 2)).astype(F32) / C)
    phase = step.astype(F32) * frequency
    return jnp.where(channel_ids % 2 == 0, jnp.sin(phase), jnp.cos(phase))


def shifted(values, step):
    if step == 0:
        return values
    columns = lax.broadcasted_iota(jnp.int32, values.shape, 1)
    width = values.shape[1]
    rolled = pltpu.roll(values, step % width, 1)
    edge = 0 if step == 1 else width - 1
    return jnp.where(columns == edge, 0.0, rolled)


def kernel(
    planes, cotangent, weights, gain, step_index,
    block_out, input_grad, weight_grad,
    columns_of, rows, cot, wf, wa, wb, wo, pre, stacks, out_a, out_b,
    sums, row_sums, ra, rb, gc,
    wacc, wpack, wsend, rz, rv, rm,
    load_sem, send_sem, recv_sem, ar_send, ar_recv, w_send, w_recv, wg_send, wg_recv, store_sem,
):
    b = lax.axis_index("band")
    p = lax.axis_index("pc")
    z, m = b // 8, b % 8
    h, k = p // 2, p % 2
    across = (b, (1 - h) * 2 + k)
    beside = (b, h * 2 + (1 - k))
    above, below = (b - 1, p), (b + 1, p)
    has_above, has_below = b > 0, b < BANDS - 1

    y, xl, parity, zh = m % 4, m // 4, z % 2, z // 2

    def band_of(z_at, xl_at, y_at):
        return (z_at * 8 + xl_at * 4 + y_at, p)

    def g_place(step, sign=1):
        dy, dz = step % 4, step // 4
        return (y + 4 + sign * dy) % 4, (zh + 4 + sign * dz) % 4

    def g_peer(step):
        place, level = g_place(step)
        return band_of(level * 2 + parity, xl, place)

    def q_place(step):
        return (xl + step % 2) % 2, (parity + step // 2) % 2

    def q_peer(step):
        side, other = q_place(step)
        return band_of(zh * 2 + other, side, y)

    def m_peer(step):
        return (z * 8 + (m + step) % 8, p)

    def z_peer(step):
        return (((z + step) % 8) * 8 + m, p)

    def load(number, src, dst):
        return pltpu.make_async_copy(src, dst, load_sem.at[number])

    loads = [load(i, planes.at[i], rows.at[0, i, pl.ds(1, 4), h, k]) for i in range(3)]
    loads.append(load(3, cotangent, cot))
    for tap_row in range(3):
        for tap_col in range(3):
            loads.append(
                load(
                    4 + 3 * tap_row + tap_col,
                    weights.at[3 * tap_row + tap_col],
                    wf.at[pl.ds(tap_col * 64, 64), pl.ds(tap_row * 256, 256)],
                )
            )
    half = pl.multiple_of(h * 128, 128)
    other_half = pl.multiple_of((1 - h) * 128, 128)
    loads.append(load(13, weights.at[:, :, pl.ds(half, 128)], wa.at[:, h, k]))
    loads.append(load(14, weights.at[:, :, pl.ds(other_half, 128)], wo))
    for copy in loads:
        copy.start()

    barrier = pltpu.get_barrier_semaphore()

    def greet(target):
        pl.semaphore_signal(barrier, inc=1, device_id=target, device_id_type=MESH)

    for step in range(1, 8):
        greet(m_peer(step))
        greet(z_peer(step))
    for step in range(1, 16):
        if step % 4 and step // 4:
            greet(g_peer(step))
    greet(q_peer(3))
    greet(across)
    greet(beside)
    far_above = jnp.logical_and(m == 0, has_above)
    far_below = jnp.logical_and(m == 7, has_below)

    @pl.when(far_above)
    def _():
        greet(above)

    @pl.when(far_below)
    def _():
        greet(below)

    def meet():
        pl.semaphore_wait(
            barrier, 26 + far_above.astype(jnp.int32) + far_below.astype(jnp.int32)
        )

    def piece(which, plane, kind, dst, src, target):
        return pltpu.make_async_remote_copy(
            src_ref=src,
            dst_ref=dst,
            send_sem=send_sem.at[which, plane, kind],
            recv_sem=recv_sem.at[which, plane, kind],
            device_id=target,
            device_id_type=MESH,
        )

    def incoming(which, plane, kind, dst, target=None):
        return piece(which, plane, kind, dst, dst, across if target is None else target)

    def send_across(which, plane):
        buf = rows.at[which, plane]
        for kind, part in ((0, buf.at[1, h, k]), (1, buf.at[4, h, k]), (2, buf.at[pl.ds(2, 2), h, k])):
            piece(which, plane, kind, part, part, across).start()

    def send_near(which, plane):
        buf = rows.at[which, plane]
        body = buf.at[pl.ds(1, 4), h, k]

        @pl.when(has_above)
        def _():
            piece(which, plane, 3, buf.at[5, h, k], buf.at[1, h, k], above).start()

        @pl.when(has_below)
        def _():
            piece(which, plane, 4, buf.at[0, h, k], buf.at[4, h, k], below).start()

        piece(which, plane, 7, body, body, beside).start()

    def pass_edges(which, plane):
        buf = rows.at[which, plane]
        first, last = buf.at[1, 1 - h, k], buf.at[4, 1 - h, k]
        incoming(which, plane, 0, first).wait_recv()

        @pl.when(has_above)
        def _():
            piece(which, plane, 5, buf.at[5, 1 - h, k], first, above).start()

        incoming(which, plane, 1, last).wait_recv()

        @pl.when(has_below)
        def _():
            piece(which, plane, 6, buf.at[0, 1 - h, k], last, below).start()

    def pass_on(which, plane):
        buf = rows.at[which, plane]
        incoming(which, plane, 2, buf.at[pl.ds(2, 2), 1 - h, k]).wait_recv()
        body = buf.at[pl.ds(1, 4), 1 - h, k]
        piece(which, plane, 8, body, body, beside).start()

    def pass_rim(which, plane):
        buf = rows.at[which, plane]

        @pl.when(has_below)
        def _():
            incoming(which, plane, 3, buf.at[5, h, k]).wait_recv()
            incoming(which, plane, 5, buf.at[5, 1 - h, k]).wait_recv()
            piece(which, plane, 9, buf.at[5, :, k], buf.at[5, :, k], beside).start()

        @pl.when(has_above)
        def _():
            incoming(which, plane, 4, buf.at[0, h, k]).wait_recv()
            incoming(which, plane, 6, buf.at[0, 1 - h, k]).wait_recv()
            piece(which, plane, 10, buf.at[0, :, k], buf.at[0, :, k], beside).start()

    def arrive(which, plane):
        buf = rows.at[which, plane]
        incoming(which, plane, 7, buf.at[pl.ds(1, 4), h, 1 - k]).wait_recv()
        incoming(which, plane, 8, buf.at[pl.ds(1, 4), 1 - h, 1 - k]).wait_recv()

        @pl.when(has_below)
        def _():
            incoming(which, plane, 9, buf.at[5, :, 1 - k]).wait_recv()

        @pl.when(has_above)
        def _():
            incoming(which, plane, 10, buf.at[0, :, 1 - k]).wait_recv()

    def settle(which, plane):
        buf = rows.at[which, plane]
        one, body = buf.at[1, h, k], buf.at[pl.ds(1, 4), h, k]
        for kind in (0, 1):
            piece(which, plane, kind, one, one, across).wait_send()
        two = buf.at[pl.ds(2, 2), h, k]
        piece(which, plane, 2, two, two, across).wait_send()
        for kind in (7, 8):
            piece(which, plane, kind, body, body, beside).wait_send()

        @pl.when(has_above)
        def _():
            for kind in (3, 5):
                piece(which, plane, kind, one, one, above).wait_send()
            piece(which, plane, 10, buf.at[0, :, k], buf.at[0, :, k], beside).wait_send()

        @pl.when(has_below)
        def _():
            for kind in (4, 6):
                piece(which, plane, kind, one, one, below).wait_send()
            piece(which, plane, 9, buf.at[5, :, k], buf.at[5, :, k], beside).wait_send()

    def ar_copy(which, stage, step, src, dst, target):
        return pltpu.make_async_remote_copy(
            src_ref=src,
            dst_ref=dst,
            send_sem=ar_send.at[which, stage, step - 1],
            recv_sem=ar_recv.at[which, stage, step - 1],
            device_id=target,
            device_id_type=MESH,
        )

    def ar_start(which):
        for step in range(1, 16):
            place, level = g_place(step)
            ar_copy(
                which, 0, step, sums.at[which, place, level // 2, level % 2],
                ra.at[which, y, zh], g_peer(step),
            ).start()
        ra[which, y, zh] = sums[which, y, zh // 2, zh % 2]

    def ar_second(which):
        for step in range(1, 16):
            place, level = g_place(step, -1)
            slot = ra.at[which, place, level]
            ar_copy(which, 0, step, slot, slot, g_peer(step)).wait_recv()
        total = None
        for i in range(4):
            for j in range(4):
                total = ra[which, i, j] if total is None else total + ra[which, i, j]
        rb[which, xl, parity] = total
        for step in range(1, 4):
            slot = rb.at[which, xl, parity]
            ar_copy(which, 1, step, slot, slot, q_peer(step)).start()

    def ar_third(which):
        for step in range(1, 4):
            side, other = q_place(step)
            slot = rb.at[which, side, other]
            ar_copy(which, 1, step, slot, slot, q_peer(step)).wait_recv()
        total = (rb[which, 0, 0] + rb[which, 0, 1]) + (rb[which, 1, 0] + rb[which, 1, 1])
        gc[which, y, zh // 2, zh % 2] = total
        for step in range(1, 16):
            slot = gc.at[which, y, zh // 2, zh % 2]
            ar_copy(which, 2, step, slot, slot, g_peer(step)).start()

    def ar_finish(which):
        for step in range(1, 16):
            place, level = g_place(step, -1)
            slot = gc.at[which, place, level // 2, level % 2]
            ar_copy(which, 2, step, slot, slot, g_peer(step)).wait_recv()

    def ar_settle(which):
        slot = gc.at[which, 0, 0, 0]
        for step in range(1, 16):
            ar_copy(which, 0, step, slot, slot, g_peer(step)).wait_send()
            ar_copy(which, 2, step, slot, slot, g_peer(step)).wait_send()
        for step in range(1, 4):
            ar_copy(which, 1, step, slot, slot, q_peer(step)).wait_send()

    columns = lax.broadcasted_iota(jnp.int32, (64, 256), 1)

    def make_sums(which):
        for plane in range(3):
            total = None
            spread = jnp.zeros((64, 256), F32)
            for i in range(4):
                values = rows[which, plane, 1 + i, h, k].astype(F32)
                total = values if total is None else total + values
                row = jnp.sum(values, axis=1, keepdims=True)
                if plane < 2:
                    row_sums[which, plane, i] = row
                else:
                    spread = jnp.where(columns == b * 4 + i, row, spread)
            for side in range(2):
                lanes = slice(side * 128, side * 128 + 128)
                sums[which, :, :, side, plane] = total[:, lanes].reshape(4, 2, 8, 128)
                if plane == 2:
                    sums[which, :, :, side, 3] = spread[:, lanes].reshape(4, 2, 8, 128)

    def totals(which, number):
        return jnp.concatenate(
            [gc[which, :, :, side, number].reshape(64, 128) for side in range(2)], axis=1
        )

    def context_row(which, plane, i, whole):
        if plane == 0:
            return row_sums[which, 1, i] + whole
        if plane == 1:
            return row_sums[which, 0, i] + whole
        own = jnp.sum(
            jnp.where(columns == b * 4 + i, totals(which, 0), 0.0), axis=1, keepdims=True
        )
        return own + whole

    whole_of = (3, 2, 1)

    def w_copy(kind, src, dst, target):
        return pltpu.make_async_remote_copy(
            src_ref=src, dst_ref=dst, send_sem=w_send.at[kind], recv_sem=w_recv.at[kind],
            device_id=target, device_id_type=MESH,
        )

    def wg_copy(stage, step, src, dst, target):
        return pltpu.make_async_remote_copy(
            src_ref=src, dst_ref=dst,
            send_sem=wg_send.at[stage, step - 1], recv_sem=wg_recv.at[stage, step - 1],
            device_id=target, device_id_type=MESH,
        )

    def convolve(which, plane, matrix, back):
        def one(i, carry):
            slab = rows[which, plane, pl.ds(i, 3)].reshape(768, 256)
            parts = jnp.dot(matrix[...], slab, preferred_element_type=F32)
            signs = (-1, 0, 1) if back else (1, 0, -1)
            total = parts[64:128]
            for tap in (0, 2):
                total = total + shifted(parts[tap * 64 : tap * 64 + 64], signs[tap])
            pre[plane, i] = total
            return carry

        lax.fori_loop(0, 4, one, 0)

    def turn_weights():
        for tap_row in range(3):
            for tap_col in range(3):
                block = wa[3 * tap_row + tap_col].reshape(256, 128).astype(F32)
                turned = jnp.transpose(block)
                turned = jnp.where(k == 0, turned[:64], turned[64:])
                wb[pl.ds(tap_col * 64, 64), pl.ds((2 - tap_row) * 256, 256)] = turned.astype(BF16)

    def finish_plane(plane):
        whole = totals(0, whole_of[plane])
        gain_vec, time_col = columns_of[0], columns_of[1]

        def finish(i, carry):
            context = context_row(0, plane, i, whole) * (1.0 / 256.0)
            act = pre[plane, i] + gain_vec * context + time_col
            gate = jax.nn.sigmoid(act)
            values = rows[0, plane, 1 + i, h, k].astype(F32)
            out_a[plane, i] = (values + act * gate).astype(BF16)
            grad = cot[plane, i].astype(F32) * gate * (1.0 + act * (1.0 - gate))
            rows[1, plane, 1 + i, h, k] = grad.astype(BF16)
            return carry

        lax.fori_loop(0, 4, finish, 0)

    def stack_plane(plane):
        def stack(i, carry):
            grad = rows[1, plane, 1 + i, h, k].astype(F32)
            for tap in range(3):
                stacks[plane, i, pl.ds(tap * 64, 64)] = shifted(grad, tap - 1).astype(BF16)
            return carry

        lax.fori_loop(0, 4, stack, 0)

    def weight_terms(plane):
        grads = jnp.concatenate([stacks[plane, i] for i in range(4)], axis=1)
        for tap_row in range(3):
            window = jnp.concatenate(
                [rows[0, plane, tap_row + i].reshape(256, 256) for i in range(4)], axis=1
            )
            term = lax.dot_general(
                window, grads, (((1,), (1,)), ((), ())), preferred_element_type=F32
            )
            if plane == 0:
                wacc[tap_row] = term
            else:
                wacc[tap_row] += term

    def wg_pack():
        for i in range(8):
            part = [wacc[tap_row, pl.ds(i * 32, 32), :] for tap_row in range(3)]
            part.append(jnp.zeros((32, 64), F32))
            block = jnp.concatenate(part, axis=1)
            for j in range(8):
                wpack[j, pl.ds(i * 4, 4)] = block[j * 4 : j * 4 + 4]
        wsend[...] = wpack[...].astype(WIRE)

    def wg_start():
        for step in range(1, 8):
            wg_copy(0, step, wsend.at[(m + step) % 8], rz.at[m], m_peer(step)).start()
        rz[m] = wsend[m]

    def wg_second():
        for step in range(1, 8):
            slot = rz.at[(m + 8 - step) % 8]
            wg_copy(0, step, slot, slot, m_peer(step)).wait_recv()
        total = rz[0].astype(F32)
        for i in range(1, 8):
            total = total + rz[i].astype(F32)
        for i in range(8):
            rv[i] = total[i * 4 : i * 4 + 4]
        for step in range(1, 8):
            wg_copy(1, step, rv.at[(z + step) % 8], rm.at[z], z_peer(step)).start()
        rm[z] = rv[z]

    def wg_finish():
        for step in range(1, 8):
            slot = rm.at[(z + 8 - step) % 8]
            wg_copy(1, step, slot, slot, z_peer(step)).wait_recv()
        total = rm[0]
        for i in range(1, 8):
            total = total + rm[i]
        for tap in range(9):
            weight_grad[tap] = total[:, tap * 64 : tap * 64 + 64]

    def wg_settle():
        for step in range(1, 8):
            wg_copy(0, step, wsend.at[0], rz.at[0], m_peer(step)).wait_send()
            wg_copy(1, step, rv.at[0], rm.at[0], z_peer(step)).wait_send()

    def make_columns():
        ids = lax.broadcasted_iota(jnp.int32, (64, 128), 0) + p * 64
        columns_of[1] = time_embed(step_index[0], ids)[:, :1]
        across_lanes = jnp.broadcast_to(gain[...].astype(F32).reshape(1, 64), (64, 64))
        same = lax.broadcasted_iota(jnp.int32, (64, 64), 0) == lax.broadcasted_iota(
            jnp.int32, (64, 64), 1
        )
        columns_of[0] = jnp.sum(jnp.where(same, across_lanes, 0.0), axis=1, keepdims=True)

    def finish_back_plane(plane):
        whole = totals(1, whole_of[plane])
        gain_vec = columns_of[0]

        def finish_back(i, carry):
            context = context_row(1, plane, i, whole) * (1.0 / 256.0)
            grad = cot[plane, i].astype(F32) + pre[plane, i] + gain_vec * context
            out_b[plane, i] = grad.astype(BF16)
            return carry

        lax.fori_loop(0, 4, finish_back, 0)

    for i in range(3):
        loads[i].wait()
    make_sums(0)
    make_columns()
    zero_row = jnp.zeros((2, 2, 64, 256), BF16)

    @pl.when(jnp.logical_not(has_above))
    def _():
        for which in range(2):
            for plane in range(3):
                rows[which, plane, 0] = zero_row

    @pl.when(jnp.logical_not(has_below))
    def _():
        for which in range(2):
            for plane in range(3):
                rows[which, plane, 5] = zero_row

    meet()
    ar_start(0)
    send_across(0, 0)
    send_across(0, 1)
    for plane in range(3):
        send_near(0, plane)
    for copy in loads[3:]:
        copy.wait()
    w_copy(1, wa.at[:, h, k], wa.at[:, h, k], beside).start()
    pass_edges(0, 0)
    ar_second(0)
    send_across(0, 2)
    pass_on(0, 0)
    pass_edges(0, 1)
    pass_on(0, 1)
    pass_rim(0, 0)
    arrive(0, 0)
    convolve(0, 0, wf, False)
    ar_third(0)
    pass_edges(0, 2)
    pass_on(0, 2)
    w_copy(0, wo, wa.at[:, h, k], across).start()
    pass_rim(0, 1)
    arrive(0, 1)
    convolve(0, 1, wf, False)
    pass_rim(0, 2)
    arrive(0, 2)
    convolve(0, 2, wf, False)

    ar_finish(0)
    finish_plane(0)
    send_across(1, 0)
    finish_plane(1)
    send_across(1, 1)
    finish_plane(2)
    make_sums(1)
    ar_start(1)
    for plane in range(3):
        send_near(1, plane)
        pltpu.make_async_copy(out_a.at[plane], block_out.at[plane], store_sem.at[0, plane]).start()
    stack_plane(0)
    weight_terms(0)
    pass_edges(1, 0)
    stack_plane(1)
    weight_terms(1)
    pass_on(1, 0)
    pass_edges(1, 1)
    stack_plane(2)
    weight_terms(2)
    ar_second(1)
    send_across(1, 2)
    pass_on(1, 1)
    wg_pack()
    wg_start()
    pass_rim(1, 0)
    arrived = wa.at[:, 1 - h, k]
    w_copy(0, arrived, arrived, across).wait_recv()
    w_copy(2, arrived, arrived, beside).start()
    pass_edges(1, 2)
    ar_third(1)
    pass_on(1, 2)
    for kind, dst in ((1, wa.at[:, h, 1 - k]), (2, wa.at[:, 1 - h, 1 - k])):
        w_copy(kind, dst, dst, beside).wait_recv()
    turn_weights()
    pass_rim(1, 1)
    arrive(1, 0)
    convolve(1, 0, wb, True)
    pass_rim(1, 2)
    arrive(1, 1)
    convolve(1, 1, wb, True)
    wg_second()
    arrive(1, 2)
    convolve(1, 2, wb, True)
    ar_finish(1)
    for plane in range(3):
        finish_back_plane(plane)
        pltpu.make_async_copy(out_b.at[plane], input_grad.at[plane], store_sem.at[1, plane]).start()
    wg_finish()

    for which in range(2):
        for plane in range(3):
            settle(which, plane)
        ar_settle(which)
    w_copy(0, wo, wo, across).wait_send()
    for kind in (1, 2):
        w_copy(kind, arrived, arrived, beside).wait_send()
    wg_settle()
    for plane in range(3):
        pltpu.make_async_copy(out_a.at[plane], block_out.at[plane], store_sem.at[0, plane]).wait()
        pltpu.make_async_copy(out_b.at[plane], input_grad.at[plane], store_sem.at[1, plane]).wait()


def place(*refs):
    sources, targets, held, sems = refs[:3], refs[3:6], refs[6:9], refs[9]
    arriving = [pltpu.make_async_copy(sources[i], held[i], sems.at[0, i]) for i in range(3)]
    leaving = [pltpu.make_async_copy(held[i], targets[i], sems.at[1, i]) for i in range(3)]
    for copy in arriving:
        copy.start()
    for i in range(3):
        arriving[i].wait()
        leaving[i].start()
    for copy in leaving:
        copy.wait()


def on_device(planes, cotangent, conv_weight, context_gain, step_index):
    anywhere = pl.BlockSpec(memory_space=pl.ANY)
    hbm = pl.BlockSpec(memory_space=pltpu.HBM)
    vmem = pl.BlockSpec(memory_space=pltpu.VMEM)
    smem = pl.BlockSpec(memory_space=pltpu.SMEM)
    dma = pltpu.SemaphoreType.DMA
    shapes = (
        jax.ShapeDtypeStruct((3, 4, 64, 256), BF16),
        jax.ShapeDtypeStruct((3, 4, 64, 256), BF16),
        jax.ShapeDtypeStruct((9, 4, 64), F32),
    )
    results = pl.pallas_call(
        kernel,
        out_shape=shapes,
        in_specs=[hbm, hbm, hbm, vmem, smem],
        out_specs=(anywhere, anywhere, vmem),
        scratch_shapes=[
            pltpu.VMEM((2, 64, 1), F32),
            pltpu.VMEM((2, 3, 6, 2, 2, 64, 256), BF16),
            pltpu.VMEM((3, 4, 64, 256), BF16),
            pltpu.VMEM((192, 768), BF16),
            pltpu.VMEM((9, 2, 2, 64, 128), BF16),
            pltpu.VMEM((192, 768), BF16),
            pltpu.VMEM((9, 64, 128), BF16),
            pltpu.VMEM((3, 4, 64, 256), F32),
            pltpu.VMEM((3, 4, 192, 256), BF16),
            pltpu.VMEM((3, 4, 64, 256), BF16),
            pltpu.VMEM((3, 4, 64, 256), BF16),
            pltpu.VMEM((2, 4, 2, 2, 4, 8, 128), F32),
            pltpu.VMEM((2, 2, 4, 64, 1), F32),
            pltpu.VMEM((2, 4, 4, 4, 8, 128), F32),
            pltpu.VMEM((2, 2, 2, 4, 8, 128), F32),
            pltpu.VMEM((2, 4, 2, 2, 4, 8, 128), F32),
            pltpu.VMEM((3, 256, 192), F32),
            pltpu.VMEM((8, 32, 640), F32),
            pltpu.VMEM((8, 32, 640), WIRE),
            pltpu.VMEM((8, 32, 640), WIRE),
            pltpu.VMEM((8, 4, 640), F32),
            pltpu.VMEM((8, 4, 640), F32),
            dma((15,)),
            dma((2, 3, 11)),
            dma((2, 3, 11)),
            dma((2, 3, 15)),
            dma((2, 3, 15)),
            dma((3,)),
            dma((3,)),
            dma((2, 7)),
            dma((2, 7)),
            dma((2, 3)),
        ],
        compiler_params=pltpu.CompilerParams(
            collective_id=0, has_side_effects=True, vmem_limit_bytes=VMEM_LIMIT
        ),
        name="triplane",
    )(planes, cotangent, conv_weight, context_gain, step_index)
    block_out, input_grad, weight_grad = pl.pallas_call(
        place,
        out_shape=shapes,
        in_specs=[anywhere] * 3,
        out_specs=(hbm, hbm, hbm),
        scratch_shapes=[pltpu.VMEM(shape.shape, shape.dtype) for shape in shapes] + [dma((2, 3))],
        compiler_params=pltpu.CompilerParams(vmem_limit_bytes=VMEM_LIMIT),
        name="place",
    )(*results)
    return block_out, input_grad, jnp.transpose(weight_grad, (0, 2, 1))


def solution(mesh):
    in_specs = (
        P(None, "band", "pc", None),
        P(None, "band", "pc", None),
        P(None, "pc", None),
        P("pc"),
        P(),
    )
    out_specs = (P(None, "band", "pc", None), P(None, "band", "pc", None), P(None, "pc", "band"))
    return jax.shard_map(
        on_device, mesh=mesh, in_specs=in_specs, out_specs=out_specs, check_vma=False
    )
```

```python
import math

import jax
import jax.numpy as jnp
from jax import lax
from jax.experimental import pallas as pl
from jax.experimental.pallas import tpu as pltpu
from jax.sharding import PartitionSpec as P

C = 256
MESH = pl.DeviceIdType.MESH
BANDS = 64
VMEM_LIMIT = 40 * 1024 * 1024
F32 = jnp.float32
BF16 = jnp.bfloat16


def time_embed(step, channel_ids):
    frequency = jnp.exp(-math.log(10000.0) * (2 * (channel_ids // 2)).astype(F32) / C)
    phase = step.astype(F32) * frequency
    return jnp.where(channel_ids % 2 == 0, jnp.sin(phase), jnp.cos(phase))


def shifted(values, step):
    if step == 0:
        return values
    columns = lax.broadcasted_iota(jnp.int32, values.shape, 1)
    width = values.shape[1]
    rolled = pltpu.roll(values, step % width, 1)
    edge = 0 if step == 1 else width - 1
    return jnp.where(columns == edge, 0.0, rolled)


def kernel(
    planes, cotangent, weights, gain, step_index,
    block_out, input_grad, weight_grad,
    columns_of, gain_row, rows, cot, wf, wa, wb, wo, pre, stacks,
    sums, row_sums, ra, rb, gc,
    wacc, wsend, rz, rv, rm,
    load_sem, send_sem, recv_sem, ar_send, ar_recv, w_send, w_recv, wg_send, wg_recv,
):
    b = lax.axis_index("band")
    p = lax.axis_index("pc")
    z, m = b // 8, b % 8
    h, k = p // 2, p % 2
    across = (b, (1 - h) * 2 + k)
    beside = (b, h * 2 + (1 - k))
    above, below = (b - 1, p), (b + 1, p)
    has_above, has_below = b > 0, b < BANDS - 1

    parity = z % 2

    def g_place(dm, dz):
        return (m + dm) % 8, (parity + dz) % 2

    def g_peer(step):
        place, side = g_place(step % 8, step // 8)
        return ((z // 2 * 2 + side) * 8 + place, p)

    def q_peer(step):
        return (((z + 2 * step) % 8) * 8 + m, p)

    def load(number, src, dst):
        return pltpu.make_async_copy(src, dst, load_sem.at[number])

    loads = [load(i, planes.at[i], rows.at[0, i, pl.ds(1, 4), h, k]) for i in range(3)]
    loads.append(load(3, cotangent, cot))
    for tap_row in range(3):
        for tap_col in range(3):
            loads.append(
                load(
                    4 + 3 * tap_row + tap_col,
                    weights.at[3 * tap_row + tap_col],
                    wf.at[pl.ds(tap_col * 64, 64), pl.ds(tap_row * 256, 256)],
                )
            )
    half = pl.multiple_of(h * 128, 128)
    other_half = pl.multiple_of((1 - h) * 128, 128)
    loads.append(load(13, weights.at[:, :, pl.ds(half, 128)], wa.at[:, h, k]))
    loads.append(load(14, weights.at[:, :, pl.ds(other_half, 128)], wo))
    gain_load = load(15, gain, gain_row)
    gain_load.start()
    for copy in loads:
        copy.start()

    barrier = pltpu.get_barrier_semaphore()

    def greet(target):
        pl.semaphore_signal(barrier, inc=1, device_id=target, device_id_type=MESH)

    for step in range(1, 4):
        greet(q_peer(step))
    for step in range(1, 16):
        greet(g_peer(step))
    greet(across)
    greet(beside)
    far_above = jnp.logical_and(jnp.logical_and(m == 0, parity == 0), has_above)
    far_below = jnp.logical_and(jnp.logical_and(m == 7, parity == 1), has_below)

    @pl.when(far_above)
    def _():
        greet(above)

    @pl.when(far_below)
    def _():
        greet(below)

    def meet():
        pl.semaphore_wait(
            barrier, 20 + far_above.astype(jnp.int32) + far_below.astype(jnp.int32)
        )

    def piece(which, plane, kind, dst, src, target):
        return pltpu.make_async_remote_copy(
            src_ref=src,
            dst_ref=dst,
            send_sem=send_sem.at[which, plane, kind],
            recv_sem=recv_sem.at[which, plane, kind],
            device_id=target,
            device_id_type=MESH,
        )

    def incoming(which, plane, kind, dst, target=None):
        return piece(which, plane, kind, dst, dst, across if target is None else target)

    def send_edges(which, plane):
        buf = rows.at[which, plane]
        for kind, part in ((0, buf.at[1, h, k]), (1, buf.at[4, h, k])):
            piece(which, plane, kind, part, part, across).start()

    def send_inner(which, plane):
        part = rows.at[which, plane, pl.ds(2, 2), h, k]
        piece(which, plane, 2, part, part, across).start()

    def send_near(which, plane):
        buf = rows.at[which, plane]
        body = buf.at[pl.ds(1, 4), h, k]

        @pl.when(has_above)
        def _():
            piece(which, plane, 3, buf.at[5, h, k], buf.at[1, h, k], above).start()

        @pl.when(has_below)
        def _():
            piece(which, plane, 4, buf.at[0, h, k], buf.at[4, h, k], below).start()

        piece(which, plane, 7, body, body, beside).start()

    def pass_edges(which, plane):
        buf = rows.at[which, plane]
        first, last = buf.at[1, 1 - h, k], buf.at[4, 1 - h, k]
        incoming(which, plane, 0, first).wait_recv()

        @pl.when(has_above)
        def _():
            piece(which, plane, 5, buf.at[5, 1 - h, k], first, above).start()

        incoming(which, plane, 1, last).wait_recv()

        @pl.when(has_below)
        def _():
            piece(which, plane, 6, buf.at[0, 1 - h, k], last, below).start()

    def pass_on(which, plane):
        buf = rows.at[which, plane]
        incoming(which, plane, 2, buf.at[pl.ds(2, 2), 1 - h, k]).wait_recv()
        body = buf.at[pl.ds(1, 4), 1 - h, k]
        piece(which, plane, 8, body, body, beside).start()

    def pass_rim(which, plane):
        buf = rows.at[which, plane]

        @pl.when(has_below)
        def _():
            incoming(which, plane, 3, buf.at[5, h, k]).wait_recv()
            incoming(which, plane, 5, buf.at[5, 1 - h, k]).wait_recv()
            piece(which, plane, 9, buf.at[5, :, k], buf.at[5, :, k], beside).start()

        @pl.when(has_above)
        def _():
            incoming(which, plane, 4, buf.at[0, h, k]).wait_recv()
            incoming(which, plane, 6, buf.at[0, 1 - h, k]).wait_recv()
            piece(which, plane, 10, buf.at[0, :, k], buf.at[0, :, k], beside).start()

    def arrive(which, plane):
        buf = rows.at[which, plane]
        incoming(which, plane, 7, buf.at[pl.ds(1, 4), h, 1 - k]).wait_recv()
        incoming(which, plane, 8, buf.at[pl.ds(1, 4), 1 - h, 1 - k]).wait_recv()

        @pl.when(has_below)
        def _():
            incoming(which, plane, 9, buf.at[5, :, 1 - k]).wait_recv()

        @pl.when(has_above)
        def _():
            incoming(which, plane, 10, buf.at[0, :, 1 - k]).wait_recv()

    def settle(which, plane):
        buf = rows.at[which, plane]
        one, body = buf.at[1, h, k], buf.at[pl.ds(1, 4), h, k]
        for kind in (0, 1):
            piece(which, plane, kind, one, one, across).wait_send()
        two = buf.at[pl.ds(2, 2), h, k]
        piece(which, plane, 2, two, two, across).wait_send()
        for kind in (7, 8):
            piece(which, plane, kind, body, body, beside).wait_send()

        @pl.when(has_above)
        def _():
            for kind in (3, 5):
                piece(which, plane, kind, one, one, above).wait_send()
            piece(which, plane, 10, buf.at[0, :, k], buf.at[0, :, k], beside).wait_send()

        @pl.when(has_below)
        def _():
            for kind in (4, 6):
                piece(which, plane, kind, one, one, below).wait_send()
            piece(which, plane, 9, buf.at[5, :, k], buf.at[5, :, k], beside).wait_send()

    def ar_copy(which, stage, step, src, dst, target):
        return pltpu.make_async_remote_copy(
            src_ref=src,
            dst_ref=dst,
            send_sem=ar_send.at[which, stage, step - 1],
            recv_sem=ar_recv.at[which, stage, step - 1],
            device_id=target,
            device_id_type=MESH,
        )

    def ar_start(which):
        for step in range(1, 16):
            place, side = g_place(step % 8, step // 8)
            ar_copy(
                which, 0, step, sums.at[which, place, side], ra.at[which, m, parity], g_peer(step)
            ).start()
        ra[which, m, parity] = sums[which, m, parity]

    def ar_second(which):
        for step in range(1, 16):
            place, side = g_place(-(step % 8) + 8, step // 8)
            slot = ra.at[which, place, side]
            ar_copy(which, 0, step, slot, slot, g_peer(step)).wait_recv()
        total = None
        for i in range(8):
            for j in range(2):
                total = ra[which, i, j] if total is None else total + ra[which, i, j]
        rb[which, z // 2] = total
        for step in range(1, 4):
            slot = rb.at[which, z // 2]
            ar_copy(which, 1, step, slot, slot, q_peer(step)).start()

    def ar_third(which):
        for step in range(1, 4):
            slot = rb.at[which, (z // 2 + 4 - step) % 4]
            ar_copy(which, 1, step, slot, slot, q_peer(step)).wait_recv()
        total = rb[which, 0]
        for i in range(1, 4):
            total = total + rb[which, i]
        gc[which, m, parity] = total
        for step in range(1, 16):
            slot = gc.at[which, m, parity]
            ar_copy(which, 2, step, slot, slot, g_peer(step)).start()

    def ar_finish(which):
        for step in range(1, 16):
            place, side = g_place(-(step % 8) + 8, step // 8)
            slot = gc.at[which, place, side]
            ar_copy(which, 2, step, slot, slot, g_peer(step)).wait_recv()

    def ar_settle(which):
        slot = gc.at[which, 0, 0]
        for step in range(1, 16):
            ar_copy(which, 0, step, slot, slot, g_peer(step)).wait_send()
            ar_copy(which, 2, step, slot, slot, g_peer(step)).wait_send()
        for step in range(1, 4):
            ar_copy(which, 1, step, slot, slot, q_peer(step)).wait_send()

    columns = lax.broadcasted_iota(jnp.int32, (64, 256), 1)

    def make_sums(which):
        for plane in range(3):
            total = None
            spread = jnp.zeros((64, 256), F32)
            for i in range(4):
                values = rows[which, plane, 1 + i, h, k].astype(F32)
                total = values if total is None else total + values
                row = jnp.sum(values, axis=1, keepdims=True)
                if plane < 2:
                    row_sums[which, plane, i] = row
                else:
                    spread = jnp.where(columns == b * 4 + i, row, spread)
            for side in range(2):
                lanes = slice(side * 128, side * 128 + 128)
                sums[which, :, side, plane] = total[:, lanes].reshape(8, 8, 128)
                if plane == 2:
                    sums[which, :, side, 3] = spread[:, lanes].reshape(8, 8, 128)

    def totals(which, number):
        return jnp.concatenate(
            [gc[which, :, side, number].reshape(64, 128) for side in range(2)], axis=1
        )

    def context_row(which, plane, i, whole):
        if plane == 0:
            return row_sums[which, 1, i] + whole
        if plane == 1:
            return row_sums[which, 0, i] + whole
        own = jnp.sum(
            jnp.where(columns == b * 4 + i, totals(which, 0), 0.0), axis=1, keepdims=True
        )
        return own + whole

    whole_of = (3, 2, 1)

    def w_copy(kind, src, dst, target):
        return pltpu.make_async_remote_copy(
            src_ref=src, dst_ref=dst, send_sem=w_send.at[kind], recv_sem=w_recv.at[kind],
            device_id=target, device_id_type=MESH,
        )

    def wg_copy(stage, step, src, dst, target):
        return pltpu.make_async_remote_copy(
            src_ref=src, dst_ref=dst,
            send_sem=wg_send.at[stage, step - 1], recv_sem=wg_recv.at[stage, step - 1],
            device_id=target, device_id_type=MESH,
        )

    def convolve(which, plane, matrix, back):
        def one(i, carry):
            slab = rows[which, plane, pl.ds(i, 3)].reshape(768, 256)
            parts = jnp.dot(matrix[...], slab, preferred_element_type=F32)
            signs = (-1, 0, 1) if back else (1, 0, -1)
            total = parts[64:128]
            for tap in (0, 2):
                total = total + shifted(parts[tap * 64 : tap * 64 + 64], signs[tap])
            pre[plane, i] = total
            return carry

        lax.fori_loop(0, 4, one, 0)

    def turn_weights():
        for tap_row in range(3):
            for tap_col in range(3):
                block = wa[3 * tap_row + tap_col].reshape(256, 128).astype(F32)
                turned = jnp.transpose(block)
                turned = jnp.where(k == 0, turned[:64], turned[64:])
                wb[pl.ds(tap_col * 64, 64), pl.ds((2 - tap_row) * 256, 256)] = turned.astype(BF16)

    def finish_plane(plane):
        whole = totals(0, whole_of[plane])
        gain_vec, time_col = columns_of[0], columns_of[1]

        def finish(i, carry):
            context = context_row(0, plane, i, whole) * (1.0 / 256.0)
            act = pre[plane, i] + gain_vec * context + time_col
            gate = jax.nn.sigmoid(act)
            values = rows[0, plane, 1 + i, h, k].astype(F32)
            block_out[plane, i] = (values + act * gate).astype(BF16)
            grad = cot[plane, i].astype(F32) * gate * (1.0 + act * (1.0 - gate))
            rows[1, plane, 1 + i, h, k] = grad.astype(BF16)
            return carry

        lax.fori_loop(0, 4, finish, 0)

    def stack_plane(plane):
        def stack(i, carry):
            grad = rows[1, plane, 1 + i, h, k].astype(F32)
            for tap in range(3):
                stacks[plane, i, pl.ds(tap * 64, 64)] = shifted(grad, tap - 1).astype(BF16)
            return carry

        lax.fori_loop(0, 4, stack, 0)

    def weight_terms(plane):
        grads = jnp.concatenate([stacks[plane, i] for i in range(4)], axis=1)
        for tap_row in range(3):
            window = jnp.concatenate(
                [rows[0, plane, tap_row + i].reshape(256, 256) for i in range(4)], axis=1
            )
            term = lax.dot_general(
                window, grads, (((1,), (1,)), ((), ())), preferred_element_type=F32
            )
            if plane == 0:
                wacc[tap_row] = term
            else:
                wacc[tap_row] += term

    def wg_pack():
        for i in range(8):
            part = [wacc[tap_row, pl.ds(i * 32, 32), :] for tap_row in range(3)]
            part.append(jnp.zeros((32, 64), F32))
            block = jnp.concatenate(part, axis=1)
            for j in range(8):
                wsend[j, i % 2, i // 2] = block[j * 4 : j * 4 + 4]

    def wg_start():
        for step in range(1, 16):
            place, side = g_place(step % 8, step // 8)
            wg_copy(0, step, wsend.at[place, side], rz.at[m, parity], g_peer(step)).start()
        rz[m, parity] = wsend[m, parity]

    def wg_second():
        for step in range(1, 16):
            place, side = g_place(-(step % 8) + 8, step // 8)
            slot = rz.at[place, side]
            wg_copy(0, step, slot, slot, g_peer(step)).wait_recv()
        total = None
        for i in range(8):
            for j in range(2):
                total = rz[i, j] if total is None else total + rz[i, j]
        rv[...] = total
        for step in range(1, 4):
            wg_copy(1, step, rv.at[(z // 2 + step) % 4], rm.at[z // 2], q_peer(step)).start()
        rm[z // 2] = rv[z // 2]

    def wg_finish():
        for step in range(1, 4):
            slot = rm.at[(z // 2 + 4 - step) % 4]
            wg_copy(1, step, slot, slot, q_peer(step)).wait_recv()
        total = rm[0]
        for i in range(1, 4):
            total = total + rm[i]
        for tap in range(9):
            weight_grad[tap] = total[:, tap * 64 : tap * 64 + 64]

    def wg_settle():
        for step in range(1, 16):
            wg_copy(0, step, wsend.at[0, 0], rz.at[0, 0], g_peer(step)).wait_send()
        for step in range(1, 4):
            wg_copy(1, step, rv.at[0], rm.at[0], q_peer(step)).wait_send()

    def make_columns():
        ids = lax.broadcasted_iota(jnp.int32, (64, 128), 0) + p * 64
        columns_of[1] = time_embed(step_index[0], ids)[:, :1]
        across_lanes = jnp.broadcast_to(gain_row[...].astype(F32).reshape(1, 64), (64, 64))
        same = lax.broadcasted_iota(jnp.int32, (64, 64), 0) == lax.broadcasted_iota(
            jnp.int32, (64, 64), 1
        )
        columns_of[0] = jnp.sum(jnp.where(same, across_lanes, 0.0), axis=1, keepdims=True)

    def finish_back_plane(plane):
        whole = totals(1, whole_of[plane])
        gain_vec = columns_of[0]

        def finish_back(i, carry):
            context = context_row(1, plane, i, whole) * (1.0 / 256.0)
            grad = cot[plane, i].astype(F32) + pre[plane, i] + gain_vec * context
            input_grad[plane, i] = grad.astype(BF16)
            return carry

        lax.fori_loop(0, 4, finish_back, 0)

    for i in range(3):
        loads[i].wait()
    make_sums(0)
    gain_load.wait()
    make_columns()
    zero_row = jnp.zeros((2, 2, 64, 256), BF16)

    @pl.when(jnp.logical_not(has_above))
    def _():
        for which in range(2):
            for plane in range(3):
                rows[which, plane, 0] = zero_row

    @pl.when(jnp.logical_not(has_below))
    def _():
        for which in range(2):
            for plane in range(3):
                rows[which, plane, 5] = zero_row

    arrived = wa.at[:, 1 - h, k]

    def loaded():
        for copy in loads[3:]:
            copy.wait()
        w_copy(1, wa.at[:, h, k], wa.at[:, h, k], beside).start()

    def w_first():
        w_copy(0, wo, wa.at[:, h, k], across).start()

    def w_forward():
        w_copy(0, arrived, arrived, across).wait_recv()
        w_copy(2, arrived, arrived, beside).start()

    def w_turn():
        for kind, dst in ((1, wa.at[:, h, 1 - k]), (2, wa.at[:, 1 - h, 1 - k])):
            w_copy(kind, dst, dst, beside).wait_recv()
        turn_weights()

    def convolve_step(which, plane):
        convolve(which, plane, wb if which else wf, which == 1)

    def weight_step(plane):
        stack_plane(plane)
        weight_terms(plane)

    meet()
    ar_start(0)
    send_edges(0, 0)
    send_edges(0, 1)
    send_edges(0, 2)
    send_inner(0, 0)
    send_inner(0, 1)
    send_inner(0, 2)
    send_near(0, 0)
    send_near(0, 1)
    send_near(0, 2)
    loaded()
    pass_edges(0, 0)
    ar_second(0)
    pass_edges(0, 1)
    pass_edges(0, 2)
    pass_rim(0, 0)
    pass_on(0, 0)
    ar_third(0)
    w_first()
    pass_rim(0, 1)
    pass_on(0, 1)
    arrive(0, 0)
    convolve_step(0, 0)
    pass_rim(0, 2)
    pass_on(0, 2)
    arrive(0, 1)
    convolve_step(0, 1)
    arrive(0, 2)
    convolve_step(0, 2)
    ar_finish(0)
    finish_plane(0)
    send_edges(1, 0)
    finish_plane(1)
    send_edges(1, 1)
    finish_plane(2)
    send_edges(1, 2)
    make_sums(1)
    ar_start(1)
    send_near(1, 0)
    send_near(1, 1)
    send_near(1, 2)
    send_inner(1, 0)
    send_inner(1, 1)
    send_inner(1, 2)
    weight_step(0)
    pass_edges(1, 0)
    weight_step(1)
    pass_edges(1, 1)
    weight_step(2)
    ar_second(1)
    pass_edges(1, 2)
    wg_pack()
    wg_start()
    pass_rim(1, 0)
    pass_on(1, 0)
    w_forward()
    w_turn()
    ar_third(1)
    pass_rim(1, 1)
    pass_on(1, 1)
    arrive(1, 0)
    convolve_step(1, 0)
    pass_rim(1, 2)
    pass_on(1, 2)
    arrive(1, 1)
    convolve_step(1, 1)
    wg_second()
    arrive(1, 2)
    convolve_step(1, 2)
    ar_finish(1)
    finish_back_plane(0)
    finish_back_plane(1)
    finish_back_plane(2)
    wg_finish()

    for which in range(2):
        for plane in range(3):
            settle(which, plane)
        ar_settle(which)
    w_copy(0, wo, wo, across).wait_send()
    for kind in (1, 2):
        w_copy(kind, arrived, arrived, beside).wait_send()
    wg_settle()


def place(*refs):
    sources, targets, sems = refs[:3], refs[3:6], refs[6]
    copies = [pltpu.make_async_copy(sources[i], targets[i], sems.at[i]) for i in range(3)]
    for copy in copies:
        copy.start()
    for copy in copies:
        copy.wait()


def on_device(planes, cotangent, conv_weight, context_gain, step_index):
    anywhere = pl.BlockSpec(memory_space=pl.ANY)
    hbm = pl.BlockSpec(memory_space=pltpu.HBM)
    vmem = pl.BlockSpec(memory_space=pltpu.VMEM)
    smem = pl.BlockSpec(memory_space=pltpu.SMEM)
    dma = pltpu.SemaphoreType.DMA
    shapes = (
        jax.ShapeDtypeStruct((3, 4, 64, 256), BF16),
        jax.ShapeDtypeStruct((3, 4, 64, 256), BF16),
        jax.ShapeDtypeStruct((9, 4, 64), F32),
    )
    def held(array):
        return pltpu.with_memory_space_constraint(array, pltpu.HBM)

    results = pl.pallas_call(
        kernel,
        out_shape=shapes,
        in_specs=[hbm, hbm, hbm, hbm, smem],
        out_specs=(vmem, vmem, vmem),
        scratch_shapes=[
            pltpu.VMEM((2, 64, 1), F32),
            pltpu.VMEM((64,), BF16),
            pltpu.VMEM((2, 3, 6, 2, 2, 64, 256), BF16),
            pltpu.VMEM((3, 4, 64, 256), BF16),
            pltpu.VMEM((192, 768), BF16),
            pltpu.VMEM((9, 2, 2, 64, 128), BF16),
            pltpu.VMEM((192, 768), BF16),
            pltpu.VMEM((9, 64, 128), BF16),
            pltpu.VMEM((3, 4, 64, 256), F32),
            pltpu.VMEM((3, 4, 192, 256), BF16),
            pltpu.VMEM((2, 8, 2, 4, 8, 128), F32),
            pltpu.VMEM((2, 2, 4, 64, 1), F32),
            pltpu.VMEM((2, 8, 2, 4, 8, 128), F32),
            pltpu.VMEM((2, 4, 4, 8, 128), F32),
            pltpu.VMEM((2, 8, 2, 4, 8, 128), F32),
            pltpu.VMEM((3, 256, 192), F32),
            pltpu.VMEM((8, 2, 4, 4, 640), F32),
            pltpu.VMEM((8, 2, 4, 4, 640), F32),
            pltpu.VMEM((4, 4, 640), F32),
            pltpu.VMEM((4, 4, 640), F32),
            dma((16,)),
            dma((2, 3, 11)),
            dma((2, 3, 11)),
            dma((2, 3, 15)),
            dma((2, 3, 15)),
            dma((3,)),
            dma((3,)),
            dma((2, 15)),
            dma((2, 15)),
        ],
        compiler_params=pltpu.CompilerParams(
            collective_id=0, has_side_effects=True, vmem_limit_bytes=VMEM_LIMIT
        ),
        name="triplane",
    )(held(planes), held(cotangent), held(conv_weight), held(context_gain), step_index)
    block_out, input_grad, weight_grad = pl.pallas_call(
        place,
        out_shape=shapes,
        in_specs=[vmem] * 3,
        out_specs=(hbm, hbm, hbm),
        scratch_shapes=[dma((3,))],
        compiler_params=pltpu.CompilerParams(vmem_limit_bytes=32 * 1024 * 1024),
        name="place",
    )(*results)
    return block_out, input_grad, jnp.transpose(weight_grad, (0, 2, 1))


def solution(mesh):
    in_specs = (
        P(None, "band", "pc", None),
        P(None, "band", "pc", None),
        P(None, "pc", None),
        P("pc"),
        P(),
    )
    out_specs = (P(None, "band", "pc", None), P(None, "band", "pc", None), P(None, "pc", "band"))
    return jax.shard_map(
        on_device, mesh=mesh, in_specs=in_specs, out_specs=out_specs, check_vma=False
    )
```

```python
import math

import jax
import jax.numpy as jnp
from jax import lax
from jax.experimental import pallas as pl
from jax.experimental.pallas import tpu as pltpu
from jax.sharding import PartitionSpec as P

C = 256
MESH = pl.DeviceIdType.MESH
BANDS = 64
VMEM_LIMIT = 40 * 1024 * 1024
F32 = jnp.float32
BF16 = jnp.bfloat16


def time_embed(step, channel_ids):
    frequency = jnp.exp(-math.log(10000.0) * (2 * (channel_ids // 2)).astype(F32) / C)
    phase = step.astype(F32) * frequency
    return jnp.where(channel_ids % 2 == 0, jnp.sin(phase), jnp.cos(phase))


def shifted(values, step):
    if step == 0:
        return values
    columns = lax.broadcasted_iota(jnp.int32, values.shape, 1)
    width = values.shape[1]
    rolled = pltpu.roll(values, step % width, 1)
    edge = 0 if step == 1 else width - 1
    return jnp.where(columns == edge, 0.0, rolled)


def kernel(
    planes, cotangent, weights, gain, step_index,
    block_out, input_grad, weight_grad,
    columns_of, gain_row, rows, cot, wf, wa, wb, wo, pre, stacks,
    sums, row_sums, ra, rb, gc, sumsb, rab, gcb,
    wacc, wsend, rz, rv, rm,
    load_sem, send_sem, recv_sem, ar_send, ar_recv, w_send, w_recv, wg_send, wg_recv,
):
    b = lax.axis_index("band")
    p = lax.axis_index("pc")
    z, m = b // 8, b % 8
    h, k = p // 2, p % 2
    across = (b, (1 - h) * 2 + k)
    beside = (b, h * 2 + (1 - k))
    above, below = (b - 1, p), (b + 1, p)
    has_above, has_below = b > 0, b < BANDS - 1

    parity = z % 2

    def g_place(dm, dz):
        return (m + dm) % 8, (parity + dz) % 2

    def g_peer(step):
        place, side = g_place(step % 8, step // 8)
        return ((z // 2 * 2 + side) * 8 + place, p)

    def q_peer(step):
        return (((z + 2 * step) % 8) * 8 + m, p)

    def load(number, src, dst):
        return pltpu.make_async_copy(src, dst, load_sem.at[number])

    loads = [load(i, planes.at[i], rows.at[0, i, pl.ds(1, 4), h, k]) for i in range(3)]
    loads.append(load(3, cotangent, cot))
    for tap_row in range(3):
        for tap_col in range(3):
            loads.append(
                load(
                    4 + 3 * tap_row + tap_col,
                    weights.at[3 * tap_row + tap_col],
                    wf.at[pl.ds(tap_col * 64, 64), pl.ds(tap_row * 256, 256)],
                )
            )
    half = pl.multiple_of(h * 128, 128)
    other_half = pl.multiple_of((1 - h) * 128, 128)
    loads.append(load(13, weights.at[:, :, pl.ds(half, 128)], wa.at[:, h, k]))
    loads.append(load(14, weights.at[:, :, pl.ds(other_half, 128)], wo))
    gain_load = load(15, gain, gain_row)
    gain_load.start()
    for copy in loads:
        copy.start()

    barrier = pltpu.get_barrier_semaphore()

    def greet(target):
        pl.semaphore_signal(barrier, inc=1, device_id=target, device_id_type=MESH)

    for step in range(1, 4):
        greet(q_peer(step))
    for step in range(1, 16):
        greet(g_peer(step))
    greet(across)
    greet(beside)
    far_above = jnp.logical_and(jnp.logical_and(m == 0, parity == 0), has_above)
    far_below = jnp.logical_and(jnp.logical_and(m == 7, parity == 1), has_below)

    @pl.when(far_above)
    def _():
        greet(above)

    @pl.when(far_below)
    def _():
        greet(below)

    def meet():
        pl.semaphore_wait(
            barrier, 20 + far_above.astype(jnp.int32) + far_below.astype(jnp.int32)
        )

    def piece(which, plane, kind, dst, src, target):
        return pltpu.make_async_remote_copy(
            src_ref=src,
            dst_ref=dst,
            send_sem=send_sem.at[which, plane, kind],
            recv_sem=recv_sem.at[which, plane, kind],
            device_id=target,
            device_id_type=MESH,
        )

    def incoming(which, plane, kind, dst, target=None):
        return piece(which, plane, kind, dst, dst, across if target is None else target)

    def send_edges(which, plane):
        buf = rows.at[which, plane]
        for kind, part in ((0, buf.at[1, h, k]), (1, buf.at[4, h, k])):
            piece(which, plane, kind, part, part, across).start()

    def send_inner(which, plane):
        part = rows.at[which, plane, pl.ds(2, 2), h, k]
        piece(which, plane, 2, part, part, across).start()

    def send_near(which, plane):
        buf = rows.at[which, plane]
        body = buf.at[pl.ds(1, 4), h, k]

        @pl.when(has_above)
        def _():
            piece(which, plane, 3, buf.at[5, h, k], buf.at[1, h, k], above).start()

        @pl.when(has_below)
        def _():
            piece(which, plane, 4, buf.at[0, h, k], buf.at[4, h, k], below).start()

        piece(which, plane, 7, body, body, beside).start()

    def pass_edges(which, plane):
        buf = rows.at[which, plane]
        first, last = buf.at[1, 1 - h, k], buf.at[4, 1 - h, k]
        incoming(which, plane, 0, first).wait_recv()

        @pl.when(has_above)
        def _():
            piece(which, plane, 5, buf.at[5, 1 - h, k], first, above).start()

        incoming(which, plane, 1, last).wait_recv()

        @pl.when(has_below)
        def _():
            piece(which, plane, 6, buf.at[0, 1 - h, k], last, below).start()

    def pass_on(which, plane):
        buf = rows.at[which, plane]
        incoming(which, plane, 2, buf.at[pl.ds(2, 2), 1 - h, k]).wait_recv()
        body = buf.at[pl.ds(1, 4), 1 - h, k]
        piece(which, plane, 8, body, body, beside).start()

    def pass_rim(which, plane):
        buf = rows.at[which, plane]

        @pl.when(has_below)
        def _():
            incoming(which, plane, 3, buf.at[5, h, k]).wait_recv()
            incoming(which, plane, 5, buf.at[5, 1 - h, k]).wait_recv()
            piece(which, plane, 9, buf.at[5, :, k], buf.at[5, :, k], beside).start()

        @pl.when(has_above)
        def _():
            incoming(which, plane, 4, buf.at[0, h, k]).wait_recv()
            incoming(which, plane, 6, buf.at[0, 1 - h, k]).wait_recv()
            piece(which, plane, 10, buf.at[0, :, k], buf.at[0, :, k], beside).start()

    def arrive(which, plane):
        buf = rows.at[which, plane]
        incoming(which, plane, 7, buf.at[pl.ds(1, 4), h, 1 - k]).wait_recv()
        incoming(which, plane, 8, buf.at[pl.ds(1, 4), 1 - h, 1 - k]).wait_recv()

        @pl.when(has_below)
        def _():
            incoming(which, plane, 9, buf.at[5, :, 1 - k]).wait_recv()

        @pl.when(has_above)
        def _():
            incoming(which, plane, 10, buf.at[0, :, 1 - k]).wait_recv()

    def settle(which, plane):
        buf = rows.at[which, plane]
        one, body = buf.at[1, h, k], buf.at[pl.ds(1, 4), h, k]
        for kind in (0, 1):
            piece(which, plane, kind, one, one, across).wait_send()
        two = buf.at[pl.ds(2, 2), h, k]
        piece(which, plane, 2, two, two, across).wait_send()
        for kind in (7, 8):
            piece(which, plane, kind, body, body, beside).wait_send()

        @pl.when(has_above)
        def _():
            for kind in (3, 5):
                piece(which, plane, kind, one, one, above).wait_send()
            piece(which, plane, 10, buf.at[0, :, k], buf.at[0, :, k], beside).wait_send()

        @pl.when(has_below)
        def _():
            for kind in (4, 6):
                piece(which, plane, kind, one, one, below).wait_send()
            piece(which, plane, 9, buf.at[5, :, k], buf.at[5, :, k], beside).wait_send()

    def ar_copy(which, stage, step, src, dst, target):
        return pltpu.make_async_remote_copy(
            src_ref=src,
            dst_ref=dst,
            send_sem=ar_send.at[which, stage, step - 1],
            recv_sem=ar_recv.at[which, stage, step - 1],
            device_id=target,
            device_id_type=MESH,
        )

    def first_slot(which, place, side):
        return ra.at[which, place, side] if which == 0 else rab.at[place, side]

    def last_slot(which, place, side):
        return gc.at[which, place, side] if which == 0 else gcb.at[place, side]

    def ar_start(which):
        if which == 1:
            sumsb[...] = sums[1].reshape(8, 2, 32, 128).astype(BF16)
        for step in range(1, 16):
            place, side = g_place(step % 8, step // 8)
            ar_copy(
                which, 0, step,
                sums.at[which, place, side] if which == 0 else sumsb.at[place, side],
                first_slot(which, m, parity), g_peer(step),
            ).start()
        if which == 0:
            ra[which, m, parity] = sums[which, m, parity]
        else:
            rab[m, parity] = sumsb[m, parity]

    def ar_second(which):
        for step in range(1, 16):
            place, side = g_place(-(step % 8) + 8, step // 8)
            slot = first_slot(which, place, side)
            ar_copy(which, 0, step, slot, slot, g_peer(step)).wait_recv()
        total = None
        for i in range(8):
            for j in range(2):
                term = ra[which, i, j] if which == 0 else rab[i, j].astype(F32)
                total = term if total is None else total + term
        rb[which, z // 2] = total.reshape(4, 8, 128)
        for step in range(1, 4):
            slot = rb.at[which, z // 2]
            ar_copy(which, 1, step, slot, slot, q_peer(step)).start()

    def ar_third(which):
        for step in range(1, 4):
            slot = rb.at[which, (z // 2 + 4 - step) % 4]
            ar_copy(which, 1, step, slot, slot, q_peer(step)).wait_recv()
        total = rb[which, 0]
        for i in range(1, 4):
            total = total + rb[which, i]
        if which == 0:
            gc[which, m, parity] = total
        else:
            gcb[m, parity] = total.reshape(32, 128).astype(BF16)
        for step in range(1, 16):
            slot = last_slot(which, m, parity)
            ar_copy(which, 2, step, slot, slot, g_peer(step)).start()

    def ar_finish(which):
        for step in range(1, 16):
            place, side = g_place(-(step % 8) + 8, step // 8)
            slot = last_slot(which, place, side)
            ar_copy(which, 2, step, slot, slot, g_peer(step)).wait_recv()

    def ar_settle(which):
        ends = last_slot(which, 0, 0)
        slot = rb.at[which, 0]
        for step in range(1, 16):
            ar_copy(which, 0, step, ends, ends, g_peer(step)).wait_send()
            ar_copy(which, 2, step, ends, ends, g_peer(step)).wait_send()
        for step in range(1, 4):
            ar_copy(which, 1, step, slot, slot, q_peer(step)).wait_send()

    columns = lax.broadcasted_iota(jnp.int32, (64, 256), 1)

    def make_sums(which):
        for plane in range(3):
            total = None
            spread = jnp.zeros((64, 256), F32)
            for i in range(4):
                values = rows[which, plane, 1 + i, h, k].astype(F32)
                total = values if total is None else total + values
                row = jnp.sum(values, axis=1, keepdims=True)
                if plane < 2:
                    row_sums[which, plane, i] = row
                else:
                    spread = jnp.where(columns == b * 4 + i, row, spread)
            for side in range(2):
                lanes = slice(side * 128, side * 128 + 128)
                sums[which, :, side, plane] = total[:, lanes].reshape(8, 8, 128)
                if plane == 2:
                    sums[which, :, side, 3] = spread[:, lanes].reshape(8, 8, 128)

    def totals(which, number):
        if which == 0:
            halves = [gc[which, :, side, number] for side in range(2)]
        else:
            at = slice(number * 8, number * 8 + 8)
            halves = [gcb[:, side].astype(F32)[:, at, :] for side in range(2)]
        return jnp.concatenate([half_of.reshape(64, 128) for half_of in halves], axis=1)

    def context_row(which, plane, i, whole):
        if plane == 0:
            return row_sums[which, 1, i] + whole
        if plane == 1:
            return row_sums[which, 0, i] + whole
        own = jnp.sum(
            jnp.where(columns == b * 4 + i, totals(which, 0), 0.0), axis=1, keepdims=True
        )
        return own + whole

    whole_of = (3, 2, 1)

    def w_copy(kind, src, dst, target):
        return pltpu.make_async_remote_copy(
            src_ref=src, dst_ref=dst, send_sem=w_send.at[kind], recv_sem=w_recv.at[kind],
            device_id=target, device_id_type=MESH,
        )

    def wg_copy(stage, step, src, dst, target):
        return pltpu.make_async_remote_copy(
            src_ref=src, dst_ref=dst,
            send_sem=wg_send.at[stage, step - 1], recv_sem=wg_recv.at[stage, step - 1],
            device_id=target, device_id_type=MESH,
        )

    def convolve(which, plane, matrix, back):
        def one(i, carry):
            slab = rows[which, plane, pl.ds(i, 3)].reshape(768, 256)
            parts = jnp.dot(matrix[...], slab, preferred_element_type=F32)
            signs = (-1, 0, 1) if back else (1, 0, -1)
            total = parts[64:128]
            for tap in (0, 2):
                total = total + shifted(parts[tap * 64 : tap * 64 + 64], signs[tap])
            pre[plane, i] = total
            return carry

        lax.fori_loop(0, 4, one, 0)

    def turn_weights():
        for tap_row in range(3):
            for tap_col in range(3):
                block = wa[3 * tap_row + tap_col].reshape(256, 128).astype(F32)
                turned = jnp.transpose(block)
                turned = jnp.where(k == 0, turned[:64], turned[64:])
                wb[pl.ds(tap_col * 64, 64), pl.ds((2 - tap_row) * 256, 256)] = turned.astype(BF16)

    def finish_plane(plane):
        whole = totals(0, whole_of[plane])
        gain_vec, time_col = columns_of[0], columns_of[1]

        def finish(i, carry):
            context = context_row(0, plane, i, whole) * (1.0 / 256.0)
            act = pre[plane, i] + gain_vec * context + time_col
            gate = jax.nn.sigmoid(act)
            values = rows[0, plane, 1 + i, h, k].astype(F32)
            block_out[plane, i] = (values + act * gate).astype(BF16)
            grad = cot[plane, i].astype(F32) * gate * (1.0 + act * (1.0 - gate))
            rows[1, plane, 1 + i, h, k] = grad.astype(BF16)
            return carry

        lax.fori_loop(0, 4, finish, 0)

    def stack_plane(plane):
        def stack(i, carry):
            grad = rows[1, plane, 1 + i, h, k].astype(F32)
            for tap in range(3):
                stacks[plane, i, pl.ds(tap * 64, 64)] = shifted(grad, tap - 1).astype(BF16)
            return carry

        lax.fori_loop(0, 4, stack, 0)

    def weight_terms(plane):
        grads = jnp.concatenate([stacks[plane, i] for i in range(4)], axis=1)
        for tap_row in range(3):
            window = jnp.concatenate(
                [rows[0, plane, tap_row + i].reshape(256, 256) for i in range(4)], axis=1
            )
            term = lax.dot_general(
                window, grads, (((1,), (1,)), ((), ())), preferred_element_type=F32
            )
            if plane == 0:
                wacc[tap_row] = term
            else:
                wacc[tap_row] += term

    def wg_pack():
        for i in range(8):
            part = [wacc[tap_row, pl.ds(i * 32, 32), :] for tap_row in range(3)]
            part.append(jnp.zeros((32, 64), F32))
            block = jnp.concatenate(part, axis=1)
            for j in range(8):
                wsend[j, i % 2, i // 2] = block[j * 4 : j * 4 + 4]

    def wg_start():
        for step in range(1, 16):
            place, side = g_place(step % 8, step // 8)
            wg_copy(0, step, wsend.at[place, side], rz.at[m, parity], g_peer(step)).start()
        rz[m, parity] = wsend[m, parity]

    def wg_second():
        for step in range(1, 16):
            place, side = g_place(-(step % 8) + 8, step // 8)
            slot = rz.at[place, side]
            wg_copy(0, step, slot, slot, g_peer(step)).wait_recv()
        total = None
        for i in range(8):
            for j in range(2):
                total = rz[i, j] if total is None else total + rz[i, j]
        rv[...] = total
        for step in range(1, 4):
            wg_copy(1, step, rv.at[(z // 2 + step) % 4], rm.at[z // 2], q_peer(step)).start()
        rm[z // 2] = rv[z // 2]

    def wg_finish():
        for step in range(1, 4):
            slot = rm.at[(z // 2 + 4 - step) % 4]
            wg_copy(1, step, slot, slot, q_peer(step)).wait_recv()
        total = rm[0]
        for i in range(1, 4):
            total = total + rm[i]
        for tap in range(9):
            weight_grad[tap] = total[:, tap * 64 : tap * 64 + 64]

    def wg_settle():
        for step in range(1, 16):
            wg_copy(0, step, wsend.at[0, 0], rz.at[0, 0], g_peer(step)).wait_send()
        for step in range(1, 4):
            wg_copy(1, step, rv.at[0], rm.at[0], q_peer(step)).wait_send()

    def make_columns():
        ids = lax.broadcasted_iota(jnp.int32, (64, 128), 0) + p * 64
        columns_of[1] = time_embed(step_index[0], ids)[:, :1]
        across_lanes = jnp.broadcast_to(gain_row[...].astype(F32).reshape(1, 64), (64, 64))
        same = lax.broadcasted_iota(jnp.int32, (64, 64), 0) == lax.broadcasted_iota(
            jnp.int32, (64, 64), 1
        )
        columns_of[0] = jnp.sum(jnp.where(same, across_lanes, 0.0), axis=1, keepdims=True)

    def finish_back_plane(plane):
        whole = totals(1, whole_of[plane])
        gain_vec = columns_of[0]

        def finish_back(i, carry):
            context = context_row(1, plane, i, whole) * (1.0 / 256.0)
            grad = cot[plane, i].astype(F32) + pre[plane, i] + gain_vec * context
            input_grad[plane, i] = grad.astype(BF16)
            return carry

        lax.fori_loop(0, 4, finish_back, 0)

    for i in range(3):
        loads[i].wait()
    make_sums(0)
    gain_load.wait()
    make_columns()
    zero_row = jnp.zeros((2, 2, 64, 256), BF16)

    @pl.when(jnp.logical_not(has_above))
    def _():
        for which in range(2):
            for plane in range(3):
                rows[which, plane, 0] = zero_row

    @pl.when(jnp.logical_not(has_below))
    def _():
        for which in range(2):
            for plane in range(3):
                rows[which, plane, 5] = zero_row

    arrived = wa.at[:, 1 - h, k]

    def loaded():
        for copy in loads[3:]:
            copy.wait()
        w_copy(1, wa.at[:, h, k], wa.at[:, h, k], beside).start()

    def w_first():
        w_copy(0, wo, wa.at[:, h, k], across).start()

    def w_forward():
        w_copy(0, arrived, arrived, across).wait_recv()
        w_copy(2, arrived, arrived, beside).start()

    def w_turn():
        for kind, dst in ((1, wa.at[:, h, 1 - k]), (2, wa.at[:, 1 - h, 1 - k])):
            w_copy(kind, dst, dst, beside).wait_recv()
        turn_weights()

    def convolve_step(which, plane):
        convolve(which, plane, wb if which else wf, which == 1)

    def weight_step(plane):
        stack_plane(plane)
        weight_terms(plane)

    meet()
    ar_start(0)
    send_edges(0, 0)
    send_edges(0, 1)
    send_edges(0, 2)
    send_inner(0, 0)
    send_inner(0, 1)
    send_inner(0, 2)
    send_near(0, 0)
    send_near(0, 1)
    send_near(0, 2)
    loaded()
    pass_edges(0, 0)
    ar_second(0)
    pass_edges(0, 1)
    pass_edges(0, 2)
    pass_rim(0, 0)
    pass_on(0, 0)
    ar_third(0)
    w_first()
    pass_rim(0, 1)
    pass_on(0, 1)
    arrive(0, 0)
    convolve_step(0, 0)
    pass_rim(0, 2)
    pass_on(0, 2)
    arrive(0, 1)
    convolve_step(0, 1)
    arrive(0, 2)
    convolve_step(0, 2)
    ar_finish(0)
    finish_plane(0)
    send_edges(1, 0)
    finish_plane(1)
    send_edges(1, 1)
    finish_plane(2)
    send_edges(1, 2)
    make_sums(1)
    ar_start(1)
    send_near(1, 0)
    send_near(1, 1)
    send_near(1, 2)
    send_inner(1, 0)
    send_inner(1, 1)
    send_inner(1, 2)
    weight_step(0)
    pass_edges(1, 0)
    weight_step(1)
    pass_edges(1, 1)
    weight_step(2)
    ar_second(1)
    pass_edges(1, 2)
    wg_pack()
    wg_start()
    pass_rim(1, 0)
    pass_on(1, 0)
    w_forward()
    w_turn()
    ar_third(1)
    pass_rim(1, 1)
    pass_on(1, 1)
    arrive(1, 0)
    convolve_step(1, 0)
    pass_rim(1, 2)
    pass_on(1, 2)
    arrive(1, 1)
    convolve_step(1, 1)
    wg_second()
    ar_finish(1)
    finish_back_plane(0)
    finish_back_plane(1)
    arrive(1, 2)
    convolve_step(1, 2)
    finish_back_plane(2)
    wg_finish()

    for which in range(2):
        for plane in range(3):
            settle(which, plane)
        ar_settle(which)
    w_copy(0, wo, wo, across).wait_send()
    for kind in (1, 2):
        w_copy(kind, arrived, arrived, beside).wait_send()
    wg_settle()


def place(*refs):
    sources, targets, sems = refs[:3], refs[3:6], refs[6]
    copies = [pltpu.make_async_copy(sources[i], targets[i], sems.at[i]) for i in range(3)]
    for copy in copies:
        copy.start()
    for copy in copies:
        copy.wait()


def on_device(planes, cotangent, conv_weight, context_gain, step_index):
    anywhere = pl.BlockSpec(memory_space=pl.ANY)
    hbm = pl.BlockSpec(memory_space=pltpu.HBM)
    vmem = pl.BlockSpec(memory_space=pltpu.VMEM)
    smem = pl.BlockSpec(memory_space=pltpu.SMEM)
    dma = pltpu.SemaphoreType.DMA
    shapes = (
        jax.ShapeDtypeStruct((3, 4, 64, 256), BF16),
        jax.ShapeDtypeStruct((3, 4, 64, 256), BF16),
        jax.ShapeDtypeStruct((9, 4, 64), F32),
    )
    def held(array):
        return pltpu.with_memory_space_constraint(array, pltpu.HBM)

    results = pl.pallas_call(
        kernel,
        out_shape=shapes,
        in_specs=[hbm, hbm, hbm, hbm, smem],
        out_specs=(vmem, vmem, vmem),
        scratch_shapes=[
            pltpu.VMEM((2, 64, 1), F32),
            pltpu.VMEM((64,), BF16),
            pltpu.VMEM((2, 3, 6, 2, 2, 64, 256), BF16),
            pltpu.VMEM((3, 4, 64, 256), BF16),
            pltpu.VMEM((192, 768), BF16),
            pltpu.VMEM((9, 2, 2, 64, 128), BF16),
            pltpu.VMEM((192, 768), BF16),
            pltpu.VMEM((9, 64, 128), BF16),
            pltpu.VMEM((3, 4, 64, 256), F32),
            pltpu.VMEM((3, 4, 192, 256), BF16),
            pltpu.VMEM((2, 8, 2, 4, 8, 128), F32),
            pltpu.VMEM((2, 2, 4, 64, 1), F32),
            pltpu.VMEM((2, 8, 2, 4, 8, 128), F32),
            pltpu.VMEM((2, 4, 4, 8, 128), F32),
            pltpu.VMEM((2, 8, 2, 4, 8, 128), F32),
            pltpu.VMEM((8, 2, 32, 128), BF16),
            pltpu.VMEM((8, 2, 32, 128), BF16),
            pltpu.VMEM((8, 2, 32, 128), BF16),
            pltpu.VMEM((3, 256, 192), F32),
            pltpu.VMEM((8, 2, 4, 4, 640), F32),
            pltpu.VMEM((8, 2, 4, 4, 640), F32),
            pltpu.VMEM((4, 4, 640), F32),
            pltpu.VMEM((4, 4, 640), F32),
            dma((16,)),
            dma((2, 3, 11)),
            dma((2, 3, 11)),
            dma((2, 3, 15)),
            dma((2, 3, 15)),
            dma((3,)),
            dma((3,)),
            dma((2, 15)),
            dma((2, 15)),
        ],
        compiler_params=pltpu.CompilerParams(
            collective_id=0, has_side_effects=True, vmem_limit_bytes=VMEM_LIMIT
        ),
        name="triplane",
    )(held(planes), held(cotangent), held(conv_weight), held(context_gain), step_index)
    block_out, input_grad, weight_grad = pl.pallas_call(
        place,
        out_shape=shapes,
        in_specs=[vmem] * 3,
        out_specs=(hbm, hbm, hbm),
        scratch_shapes=[dma((3,))],
        compiler_params=pltpu.CompilerParams(vmem_limit_bytes=32 * 1024 * 1024),
        name="place",
    )(*results)
    return block_out, input_grad, jnp.transpose(weight_grad, (0, 2, 1))


def solution(mesh):
    in_specs = (
        P(None, "band", "pc", None),
        P(None, "band", "pc", None),
        P(None, "pc", None),
        P("pc"),
        P(),
    )
    out_specs = (P(None, "band", "pc", None), P(None, "band", "pc", None), P(None, "pc", "band"))
    return jax.shard_map(
        on_device, mesh=mesh, in_specs=in_specs, out_specs=out_specs, check_vma=False
    )
```

```python
import math

import jax
import jax.numpy as jnp
from jax import lax
from jax.experimental import pallas as pl
from jax.experimental.pallas import tpu as pltpu
from jax.sharding import PartitionSpec as P

C = 256
MESH = pl.DeviceIdType.MESH
BANDS = 64
VMEM_LIMIT = 40 * 1024 * 1024
F32 = jnp.float32
BF16 = jnp.bfloat16


def time_embed(step, channel_ids):
    frequency = jnp.exp(-math.log(10000.0) * (2 * (channel_ids // 2)).astype(F32) / C)
    phase = step.astype(F32) * frequency
    return jnp.where(channel_ids % 2 == 0, jnp.sin(phase), jnp.cos(phase))


def shifted(values, step):
    if step == 0:
        return values
    columns = lax.broadcasted_iota(jnp.int32, values.shape, 1)
    width = values.shape[1]
    rolled = pltpu.roll(values, step % width, 1)
    edge = 0 if step == 1 else width - 1
    return jnp.where(columns == edge, 0.0, rolled)


def kernel(
    planes, cotangent, weights, gain, step_index,
    block_out, input_grad, weight_grad,
    columns_of, gain_row, rows, cot, wf, wa, wb, wo, pre, stacks,
    sums, row_sums, ra, rb, gc, sumsb, rab, gcb,
    wacc, wsend, rz, rv, rm,
    load_sem, send_sem, recv_sem, ar_send, ar_recv, w_send, w_recv, wg_send, wg_recv,
):
    b = lax.axis_index("band")
    p = lax.axis_index("pc")
    z, m = b // 8, b % 8
    h, k = p // 2, p % 2
    across = (b, (1 - h) * 2 + k)
    beside = (b, h * 2 + (1 - k))
    above, below = (b - 1, p), (b + 1, p)
    has_above, has_below = b > 0, b < BANDS - 1

    parity = z % 2

    def g_place(dm, dz):
        return (m + dm) % 8, (parity + dz) % 2

    def g_peer(step):
        place, side = g_place(step % 8, step // 8)
        return ((z // 2 * 2 + side) * 8 + place, p)

    def q_peer(step):
        return (((z + 2 * step) % 8) * 8 + m, p)

    def load(number, src, dst):
        return pltpu.make_async_copy(src, dst, load_sem.at[number])

    loads = [load(i, planes.at[i], rows.at[0, i, pl.ds(1, 4), h, k]) for i in range(3)]
    loads.append(load(3, cotangent, cot))
    for tap_row in range(3):
        for tap_col in range(3):
            loads.append(
                load(
                    4 + 3 * tap_row + tap_col,
                    weights.at[3 * tap_row + tap_col],
                    wf.at[pl.ds(tap_col * 64, 64), pl.ds(tap_row * 256, 256)],
                )
            )
    half = pl.multiple_of(h * 128, 128)
    other_half = pl.multiple_of((1 - h) * 128, 128)
    loads.append(load(13, weights.at[:, :, pl.ds(half, 128)], wa.at[:, h, k]))
    loads.append(load(14, weights.at[:, :, pl.ds(other_half, 128)], wo))
    gain_load = load(15, gain, gain_row)
    gain_load.start()
    for copy in loads:
        copy.start()

    barrier = pltpu.get_barrier_semaphore()

    def greet(target):
        pl.semaphore_signal(barrier, inc=1, device_id=target, device_id_type=MESH)

    for step in range(1, 4):
        greet(q_peer(step))
    for step in range(1, 16):
        greet(g_peer(step))
    greet(across)
    greet(beside)
    far_above = jnp.logical_and(jnp.logical_and(m == 0, parity == 0), has_above)
    far_below = jnp.logical_and(jnp.logical_and(m == 7, parity == 1), has_below)

    @pl.when(far_above)
    def _():
        greet(above)

    @pl.when(far_below)
    def _():
        greet(below)

    def meet():
        pl.semaphore_wait(
            barrier, 20 + far_above.astype(jnp.int32) + far_below.astype(jnp.int32)
        )

    def piece(which, plane, kind, dst, src, target):
        return pltpu.make_async_remote_copy(
            src_ref=src,
            dst_ref=dst,
            send_sem=send_sem.at[which, plane, kind],
            recv_sem=recv_sem.at[which, plane, kind],
            device_id=target,
            device_id_type=MESH,
        )

    def incoming(which, plane, kind, dst, target=None):
        return piece(which, plane, kind, dst, dst, across if target is None else target)

    def send_edges(which, plane):
        buf = rows.at[which, plane]
        for kind, part in ((0, buf.at[1, h, k]), (1, buf.at[4, h, k])):
            piece(which, plane, kind, part, part, across).start()

    def send_inner(which, plane):
        part = rows.at[which, plane, pl.ds(2, 2), h, k]
        piece(which, plane, 2, part, part, across).start()

    def send_near(which, plane):
        buf = rows.at[which, plane]
        body = buf.at[pl.ds(1, 4), h, k]

        @pl.when(has_above)
        def _():
            piece(which, plane, 3, buf.at[5, h, k], buf.at[1, h, k], above).start()

        @pl.when(has_below)
        def _():
            piece(which, plane, 4, buf.at[0, h, k], buf.at[4, h, k], below).start()

        piece(which, plane, 7, body, body, beside).start()

    def pass_edges(which, plane):
        buf = rows.at[which, plane]
        first, last = buf.at[1, 1 - h, k], buf.at[4, 1 - h, k]
        incoming(which, plane, 0, first).wait_recv()

        @pl.when(has_above)
        def _():
            piece(which, plane, 5, buf.at[5, 1 - h, k], first, above).start()

        incoming(which, plane, 1, last).wait_recv()

        @pl.when(has_below)
        def _():
            piece(which, plane, 6, buf.at[0, 1 - h, k], last, below).start()

    def pass_on(which, plane):
        buf = rows.at[which, plane]
        incoming(which, plane, 2, buf.at[pl.ds(2, 2), 1 - h, k]).wait_recv()
        body = buf.at[pl.ds(1, 4), 1 - h, k]
        piece(which, plane, 8, body, body, beside).start()

    def pass_rim(which, plane):
        buf = rows.at[which, plane]

        @pl.when(has_below)
        def _():
            incoming(which, plane, 3, buf.at[5, h, k]).wait_recv()
            incoming(which, plane, 5, buf.at[5, 1 - h, k]).wait_recv()
            piece(which, plane, 9, buf.at[5, :, k], buf.at[5, :, k], beside).start()

        @pl.when(has_above)
        def _():
            incoming(which, plane, 4, buf.at[0, h, k]).wait_recv()
            incoming(which, plane, 6, buf.at[0, 1 - h, k]).wait_recv()
            piece(which, plane, 10, buf.at[0, :, k], buf.at[0, :, k], beside).start()

    def arrive(which, plane):
        buf = rows.at[which, plane]
        incoming(which, plane, 7, buf.at[pl.ds(1, 4), h, 1 - k]).wait_recv()
        incoming(which, plane, 8, buf.at[pl.ds(1, 4), 1 - h, 1 - k]).wait_recv()

        @pl.when(has_below)
        def _():
            incoming(which, plane, 9, buf.at[5, :, 1 - k]).wait_recv()

        @pl.when(has_above)
        def _():
            incoming(which, plane, 10, buf.at[0, :, 1 - k]).wait_recv()

    def settle(which, plane):
        buf = rows.at[which, plane]
        one, body = buf.at[1, h, k], buf.at[pl.ds(1, 4), h, k]
        for kind in (0, 1):
            piece(which, plane, kind, one, one, across).wait_send()
        two = buf.at[pl.ds(2, 2), h, k]
        piece(which, plane, 2, two, two, across).wait_send()
        for kind in (7, 8):
            piece(which, plane, kind, body, body, beside).wait_send()

        @pl.when(has_above)
        def _():
            for kind in (3, 5):
                piece(which, plane, kind, one, one, above).wait_send()
            piece(which, plane, 10, buf.at[0, :, k], buf.at[0, :, k], beside).wait_send()

        @pl.when(has_below)
        def _():
            for kind in (4, 6):
                piece(which, plane, kind, one, one, below).wait_send()
            piece(which, plane, 9, buf.at[5, :, k], buf.at[5, :, k], beside).wait_send()

    def ar_copy(which, stage, step, src, dst, target):
        return pltpu.make_async_remote_copy(
            src_ref=src,
            dst_ref=dst,
            send_sem=ar_send.at[which, stage, step - 1],
            recv_sem=ar_recv.at[which, stage, step - 1],
            device_id=target,
            device_id_type=MESH,
        )

    def first_slot(which, place, side):
        return ra.at[which, place, side] if which == 0 else rab.at[place, side]

    def last_slot(which, place, side):
        return gc.at[which, place, side] if which == 0 else gcb.at[place, side]

    def ar_start(which):
        if which == 1:
            sumsb[...] = sums[1].reshape(8, 2, 32, 128).astype(BF16)
        for step in range(1, 16):
            place, side = g_place(step % 8, step // 8)
            ar_copy(
                which, 0, step,
                sums.at[which, place, side] if which == 0 else sumsb.at[place, side],
                first_slot(which, m, parity), g_peer(step),
            ).start()
        if which == 0:
            ra[which, m, parity] = sums[which, m, parity]
        else:
            rab[m, parity] = sumsb[m, parity]

    def ar_second(which):
        for step in range(1, 16):
            place, side = g_place(-(step % 8) + 8, step // 8)
            slot = first_slot(which, place, side)
            ar_copy(which, 0, step, slot, slot, g_peer(step)).wait_recv()
        total = None
        for i in range(8):
            for j in range(2):
                term = ra[which, i, j] if which == 0 else rab[i, j].astype(F32)
                total = term if total is None else total + term
        rb[which, z // 2] = total.reshape(4, 8, 128)
        for step in range(1, 4):
            slot = rb.at[which, z // 2]
            ar_copy(which, 1, step, slot, slot, q_peer(step)).start()

    def ar_third(which):
        for step in range(1, 4):
            slot = rb.at[which, (z // 2 + 4 - step) % 4]
            ar_copy(which, 1, step, slot, slot, q_peer(step)).wait_recv()
        total = rb[which, 0]
        for i in range(1, 4):
            total = total + rb[which, i]
        if which == 0:
            gc[which, m, parity] = total
        else:
            gcb[m, parity] = total.reshape(32, 128).astype(BF16)
        for step in range(1, 16):
            slot = last_slot(which, m, parity)
            ar_copy(which, 2, step, slot, slot, g_peer(step)).start()

    def ar_finish(which):
        for step in range(1, 16):
            place, side = g_place(-(step % 8) + 8, step // 8)
            slot = last_slot(which, place, side)
            ar_copy(which, 2, step, slot, slot, g_peer(step)).wait_recv()

    def ar_settle(which):
        ends = last_slot(which, 0, 0)
        slot = rb.at[which, 0]
        for step in range(1, 16):
            ar_copy(which, 0, step, ends, ends, g_peer(step)).wait_send()
            ar_copy(which, 2, step, ends, ends, g_peer(step)).wait_send()
        for step in range(1, 4):
            ar_copy(which, 1, step, slot, slot, q_peer(step)).wait_send()

    columns = lax.broadcasted_iota(jnp.int32, (64, 256), 1)

    def make_sums(which):
        for plane in range(3):
            total = None
            spread = jnp.zeros((64, 256), F32)
            for i in range(4):
                values = rows[which, plane, 1 + i, h, k].astype(F32)
                total = values if total is None else total + values
                row = jnp.sum(values, axis=1, keepdims=True)
                if plane < 2:
                    row_sums[which, plane, i] = row
                else:
                    spread = jnp.where(columns == b * 4 + i, row, spread)
            for side in range(2):
                lanes = slice(side * 128, side * 128 + 128)
                sums[which, :, side, plane] = total[:, lanes].reshape(8, 8, 128)
                if plane == 2:
                    sums[which, :, side, 3] = spread[:, lanes].reshape(8, 8, 128)

    def totals(which, number):
        if which == 0:
            halves = [gc[which, :, side, number] for side in range(2)]
        else:
            at = slice(number * 8, number * 8 + 8)
            halves = [gcb[:, side].astype(F32)[:, at, :] for side in range(2)]
        return jnp.concatenate([half_of.reshape(64, 128) for half_of in halves], axis=1)

    def context_row(which, plane, i, whole):
        if plane == 0:
            return row_sums[which, 1, i] + whole
        if plane == 1:
            return row_sums[which, 0, i] + whole
        own = jnp.sum(
            jnp.where(columns == b * 4 + i, totals(which, 0), 0.0), axis=1, keepdims=True
        )
        return own + whole

    whole_of = (3, 2, 1)

    def w_copy(kind, src, dst, target):
        return pltpu.make_async_remote_copy(
            src_ref=src, dst_ref=dst, send_sem=w_send.at[kind], recv_sem=w_recv.at[kind],
            device_id=target, device_id_type=MESH,
        )

    def wg_copy(stage, step, src, dst, target):
        return pltpu.make_async_remote_copy(
            src_ref=src, dst_ref=dst,
            send_sem=wg_send.at[stage, step - 1], recv_sem=wg_recv.at[stage, step - 1],
            device_id=target, device_id_type=MESH,
        )

    def convolve(which, plane, matrix, back):
        def one(i, carry):
            slab = rows[which, plane, pl.ds(i, 3)].reshape(768, 256)
            parts = jnp.dot(matrix[...], slab, preferred_element_type=F32)
            signs = (-1, 0, 1) if back else (1, 0, -1)
            total = parts[64:128]
            for tap in (0, 2):
                total = total + shifted(parts[tap * 64 : tap * 64 + 64], signs[tap])
            pre[plane, i] = total
            return carry

        lax.fori_loop(0, 4, one, 0)

    def turn_weights():
        for tap_row in range(3):
            for tap_col in range(3):
                block = wa[3 * tap_row + tap_col].reshape(256, 128).astype(F32)
                turned = jnp.transpose(block)
                turned = jnp.where(k == 0, turned[:64], turned[64:])
                wb[pl.ds(tap_col * 64, 64), pl.ds((2 - tap_row) * 256, 256)] = turned.astype(BF16)

    def finish_plane(plane):
        whole = totals(0, whole_of[plane])
        gain_vec, time_col = columns_of[0], columns_of[1]

        def finish(i, carry):
            context = context_row(0, plane, i, whole) * (1.0 / 256.0)
            act = pre[plane, i] + gain_vec * context + time_col
            gate = jax.nn.sigmoid(act)
            values = rows[0, plane, 1 + i, h, k].astype(F32)
            block_out[plane, i] = (values + act * gate).astype(BF16)
            grad = cot[plane, i].astype(F32) * gate * (1.0 + act * (1.0 - gate))
            rows[1, plane, 1 + i, h, k] = grad.astype(BF16)
            return carry

        lax.fori_loop(0, 4, finish, 0)

    def stack_plane(plane):
        def stack(i, carry):
            grad = rows[1, plane, 1 + i, h, k].astype(F32)
            for tap in range(3):
                stacks[plane, i, pl.ds(tap * 64, 64)] = shifted(grad, tap - 1).astype(BF16)
            return carry

        lax.fori_loop(0, 4, stack, 0)

    def weight_terms(plane):
        grads = jnp.concatenate([stacks[plane, i] for i in range(4)], axis=1)
        for tap_row in range(3):
            window = jnp.concatenate(
                [rows[0, plane, tap_row + i].reshape(256, 256) for i in range(4)], axis=1
            )
            term = lax.dot_general(
                window, grads, (((1,), (1,)), ((), ())), preferred_element_type=F32
            )
            if plane == 0:
                wacc[tap_row] = term
            else:
                wacc[tap_row] += term

    def wg_pack():
        for i in range(8):
            part = [wacc[tap_row, pl.ds(i * 32, 32), :] for tap_row in range(3)]
            part.append(jnp.zeros((32, 64), F32))
            block = jnp.concatenate(part, axis=1)
            for j in range(8):
                wsend[j, i % 2, i // 2] = block[j * 4 : j * 4 + 4]

    def wg_start():
        for step in range(1, 16):
            place, side = g_place(step % 8, step // 8)
            wg_copy(0, step, wsend.at[place, side], rz.at[m, parity], g_peer(step)).start()
        rz[m, parity] = wsend[m, parity]

    def wg_second():
        for step in range(1, 16):
            place, side = g_place(-(step % 8) + 8, step // 8)
            slot = rz.at[place, side]
            wg_copy(0, step, slot, slot, g_peer(step)).wait_recv()
        total = None
        for i in range(8):
            for j in range(2):
                total = rz[i, j] if total is None else total + rz[i, j]
        rv[...] = total
        for step in range(1, 4):
            wg_copy(1, step, rv.at[(z // 2 + step) % 4], rm.at[z // 2], q_peer(step)).start()
        rm[z // 2] = rv[z // 2]

    def wg_finish():
        for step in range(1, 4):
            slot = rm.at[(z // 2 + 4 - step) % 4]
            wg_copy(1, step, slot, slot, q_peer(step)).wait_recv()
        total = rm[0]
        for i in range(1, 4):
            total = total + rm[i]
        for tap in range(9):
            weight_grad[tap] = total[:, tap * 64 : tap * 64 + 64]

    def wg_settle():
        for step in range(1, 16):
            wg_copy(0, step, wsend.at[0, 0], rz.at[0, 0], g_peer(step)).wait_send()
        for step in range(1, 4):
            wg_copy(1, step, rv.at[0], rm.at[0], q_peer(step)).wait_send()

    def make_columns():
        ids = lax.broadcasted_iota(jnp.int32, (64, 128), 0) + p * 64
        columns_of[1] = time_embed(step_index[0], ids)[:, :1]
        across_lanes = jnp.broadcast_to(gain_row[...].astype(F32).reshape(1, 64), (64, 64))
        same = lax.broadcasted_iota(jnp.int32, (64, 64), 0) == lax.broadcasted_iota(
            jnp.int32, (64, 64), 1
        )
        columns_of[0] = jnp.sum(jnp.where(same, across_lanes, 0.0), axis=1, keepdims=True)

    def finish_back_plane(plane):
        whole = totals(1, whole_of[plane])
        gain_vec = columns_of[0]

        def finish_back(i, carry):
            context = context_row(1, plane, i, whole) * (1.0 / 256.0)
            grad = cot[plane, i].astype(F32) + pre[plane, i] + gain_vec * context
            input_grad[plane, i] = grad.astype(BF16)
            return carry

        lax.fori_loop(0, 4, finish_back, 0)

    for i in range(3):
        loads[i].wait()
    make_sums(0)
    gain_load.wait()
    make_columns()
    zero_row = jnp.zeros((2, 2, 64, 256), BF16)

    @pl.when(jnp.logical_not(has_above))
    def _():
        for which in range(2):
            for plane in range(3):
                rows[which, plane, 0] = zero_row

    @pl.when(jnp.logical_not(has_below))
    def _():
        for which in range(2):
            for plane in range(3):
                rows[which, plane, 5] = zero_row

    arrived = wa.at[:, 1 - h, k]

    def loaded():
        for copy in loads[3:]:
            copy.wait()
        w_copy(1, wa.at[:, h, k], wa.at[:, h, k], beside).start()

    def w_first():
        w_copy(0, wo, wa.at[:, h, k], across).start()

    def w_forward():
        w_copy(0, arrived, arrived, across).wait_recv()
        w_copy(2, arrived, arrived, beside).start()

    def w_turn():
        for kind, dst in ((1, wa.at[:, h, 1 - k]), (2, wa.at[:, 1 - h, 1 - k])):
            w_copy(kind, dst, dst, beside).wait_recv()
        turn_weights()

    def convolve_step(which, plane):
        convolve(which, plane, wb if which else wf, which == 1)

    def weight_step(plane):
        stack_plane(plane)
        weight_terms(plane)

    meet()
    ar_start(0)
    send_edges(0, 0)
    send_edges(0, 1)
    send_edges(0, 2)
    send_inner(0, 0)
    send_inner(0, 1)
    send_inner(0, 2)
    send_near(0, 0)
    send_near(0, 1)
    send_near(0, 2)
    loaded()
    pass_edges(0, 0)
    ar_second(0)
    pass_edges(0, 1)
    pass_edges(0, 2)
    pass_rim(0, 0)
    pass_on(0, 0)
    ar_third(0)
    w_first()
    pass_rim(0, 1)
    pass_on(0, 1)
    arrive(0, 0)
    convolve_step(0, 0)
    pass_rim(0, 2)
    pass_on(0, 2)
    arrive(0, 1)
    convolve_step(0, 1)
    arrive(0, 2)
    convolve_step(0, 2)
    ar_finish(0)
    finish_plane(0)
    send_edges(1, 0)
    finish_plane(1)
    finish_plane(2)
    make_sums(1)
    ar_start(1)
    send_edges(1, 1)
    send_edges(1, 2)
    send_near(1, 0)
    send_near(1, 1)
    send_near(1, 2)
    send_inner(1, 0)
    send_inner(1, 1)
    send_inner(1, 2)
    weight_step(0)
    pass_edges(1, 0)
    weight_step(1)
    pass_edges(1, 1)
    weight_step(2)
    ar_second(1)
    pass_edges(1, 2)
    wg_pack()
    wg_start()
    pass_rim(1, 0)
    pass_on(1, 0)
    w_forward()
    w_turn()
    ar_third(1)
    pass_rim(1, 1)
    pass_on(1, 1)
    arrive(1, 0)
    convolve_step(1, 0)
    pass_rim(1, 2)
    pass_on(1, 2)
    arrive(1, 1)
    convolve_step(1, 1)
    wg_second()
    ar_finish(1)
    finish_back_plane(0)
    finish_back_plane(1)
    arrive(1, 2)
    convolve_step(1, 2)
    finish_back_plane(2)
    wg_finish()

    for which in range(2):
        for plane in range(3):
            settle(which, plane)
        ar_settle(which)
    w_copy(0, wo, wo, across).wait_send()
    for kind in (1, 2):
        w_copy(kind, arrived, arrived, beside).wait_send()
    wg_settle()


def place(*refs):
    sources, targets, sems = refs[:3], refs[3:6], refs[6]
    copies = [pltpu.make_async_copy(sources[i], targets[i], sems.at[i]) for i in range(3)]
    for copy in copies:
        copy.start()
    for copy in copies:
        copy.wait()


def on_device(planes, cotangent, conv_weight, context_gain, step_index):
    anywhere = pl.BlockSpec(memory_space=pl.ANY)
    hbm = pl.BlockSpec(memory_space=pltpu.HBM)
    vmem = pl.BlockSpec(memory_space=pltpu.VMEM)
    smem = pl.BlockSpec(memory_space=pltpu.SMEM)
    dma = pltpu.SemaphoreType.DMA
    shapes = (
        jax.ShapeDtypeStruct((3, 4, 64, 256), BF16),
        jax.ShapeDtypeStruct((3, 4, 64, 256), BF16),
        jax.ShapeDtypeStruct((9, 4, 64), F32),
    )
    def held(array):
        return pltpu.with_memory_space_constraint(array, pltpu.HBM)

    results = pl.pallas_call(
        kernel,
        out_shape=shapes,
        in_specs=[hbm, hbm, hbm, hbm, smem],
        out_specs=(vmem, vmem, vmem),
        scratch_shapes=[
            pltpu.VMEM((2, 64, 1), F32),
            pltpu.VMEM((64,), BF16),
            pltpu.VMEM((2, 3, 6, 2, 2, 64, 256), BF16),
            pltpu.VMEM((3, 4, 64, 256), BF16),
            pltpu.VMEM((192, 768), BF16),
            pltpu.VMEM((9, 2, 2, 64, 128), BF16),
            pltpu.VMEM((192, 768), BF16),
            pltpu.VMEM((9, 64, 128), BF16),
            pltpu.VMEM((3, 4, 64, 256), F32),
            pltpu.VMEM((3, 4, 192, 256), BF16),
            pltpu.VMEM((2, 8, 2, 4, 8, 128), F32),
            pltpu.VMEM((2, 2, 4, 64, 1), F32),
            pltpu.VMEM((2, 8, 2, 4, 8, 128), F32),
            pltpu.VMEM((2, 4, 4, 8, 128), F32),
            pltpu.VMEM((2, 8, 2, 4, 8, 128), F32),
            pltpu.VMEM((8, 2, 32, 128), BF16),
            pltpu.VMEM((8, 2, 32, 128), BF16),
            pltpu.VMEM((8, 2, 32, 128), BF16),
            pltpu.VMEM((3, 256, 192), F32),
            pltpu.VMEM((8, 2, 4, 4, 640), F32),
            pltpu.VMEM((8, 2, 4, 4, 640), F32),
            pltpu.VMEM((4, 4, 640), F32),
            pltpu.VMEM((4, 4, 640), F32),
            dma((16,)),
            dma((2, 3, 11)),
            dma((2, 3, 11)),
            dma((2, 3, 15)),
            dma((2, 3, 15)),
            dma((3,)),
            dma((3,)),
            dma((2, 15)),
            dma((2, 15)),
        ],
        compiler_params=pltpu.CompilerParams(
            collective_id=0, has_side_effects=True, vmem_limit_bytes=VMEM_LIMIT
        ),
        name="triplane",
    )(held(planes), held(cotangent), held(conv_weight), held(context_gain), step_index)
    block_out, input_grad, weight_grad = pl.pallas_call(
        place,
        out_shape=shapes,
        in_specs=[vmem] * 3,
        out_specs=(hbm, hbm, hbm),
        scratch_shapes=[dma((3,))],
        compiler_params=pltpu.CompilerParams(vmem_limit_bytes=32 * 1024 * 1024),
        name="place",
    )(*results)
    return block_out, input_grad, jnp.transpose(weight_grad, (0, 2, 1))


def solution(mesh):
    in_specs = (
        P(None, "band", "pc", None),
        P(None, "band", "pc", None),
        P(None, "pc", None),
        P("pc"),
        P(),
    )
    out_specs = (P(None, "band", "pc", None), P(None, "band", "pc", None), P(None, "pc", "band"))
    return jax.shard_map(
        on_device, mesh=mesh, in_specs=in_specs, out_specs=out_specs, check_vma=False
    )
```
